256 devices in a mesh: swap: 2 (over core), ep: 128 (over x, z, y).
Axes of the slice: x: 4, y: 4, z: 8, core: 2. Of those that a mesh axis runs over, the one named last changes fastest.
Arguments:
- grad_out: bfloat16 [16384, 6144], P('ep'), may hold values from -6 to 6
- parked_inputs: bfloat16 [2, 16384, 3072], P('swap', 'ep'), may hold values from -6 to 6
- route_ids: int32 [16384, 2], P('ep'), may hold values from 0 to 7, all different within a row; in each aligned block of 128 rows (0 to 127, 128 to 255, ...) at most 34 rows name the same one
- route_probs: float32 [16384, 2], P('ep'), may hold values from 0.1 to 0.9
- flight_expert: int32 [1], replicated, may hold values from 0 to 7
- w_gate: bfloat16 [6144, 8192], P(None, 'ep'), may hold values from -0.078125 to 0.078125
- w_up: bfloat16 [6144, 8192], P(None, 'ep'), may hold values from -0.078125 to 0.078125
- w_down: bfloat16 [8192, 6144], P('ep'), may hold values from -0.0625 to 0.0625
Outputs:
- grad_in: bfloat16 [16384, 6144], P('ep', 'swap')
The draws below stay inside these ranges and needn't reach their ends.
Inputs may be any that keep to these rules, and one draw needn't show every extreme that they name: `route_ids`: each row names 2 different experts; the rows of one device name any one expert at most 34 times.
All inputs are finite; a program needn't handle non-finite values.
Results may differ from the reference program's by a relative error of at most 0.0024.
Values may be sent and summed in bfloat16 or wider, within the bound.
A program may use at most 128 MiB of HBM per device.

```python
import math
import jax
import jax.numpy as jnp
import numpy as np
from jax import lax

D = 6144
EXPERTS = 8
TOPK = 2
FF = 8192
TOK = 128
CAP = 34
TOKENS = 16384
HALF = 3072
N_EP = 128


def steps_of(stream_key, shape, pieces, least, top_value):
    loudness = 1.0
    for axis_at, blocks in pieces:
        heights = jax.random.uniform(jax.random.fold_in(jax.random.fold_in(stream_key, 6), axis_at), (blocks,), jnp.float32, least / len(pieces), top_value / len(pieces))
        loudness = loudness * jnp.repeat(jnp.exp(heights), shape[axis_at] // blocks).reshape((-1,) + (1,) * (len(shape) - 1 - axis_at))
    return loudness


def shared_out(own_key, own, number, rows, number_of, top, bound, skew):
    ranking = jax.random.permutation(own_key, number_of)
    heavy_load, common = portions_of(number_of, rows * top, bound, skew, True), portions_of(number_of, rows * top, bound, skew, False)
    places = jnp.arange(number_of)

    def named(sizes, turn):
        used = int((sizes > 0).sum())
        fixed = max(1, used // 4)
        shifted = fixed + (places - fixed + turn * (used - fixed)) % max(1, number_of - fixed)
        return jnp.zeros((number_of,), jnp.int32).at[ranking[jnp.where(places < fixed, places, shifted)]].set(jnp.asarray(sizes, jnp.int32))

    sizes = jnp.where(number % 4 == 0, named(heavy_load, number // 4), named(common, number - number // 4 - 1))
    mixed = jax.random.permutation(jax.random.fold_in(own, 3), number_of)
    giver, taker = mixed[0:number_of // 2 * 2:2], mixed[1:number_of // 2 * 2:2]
    slack = jnp.minimum(sizes[giver] - 1, bound - sizes[taker]) // 2
    slack = jnp.where((giver == ranking[0]) | (taker == ranking[0]) | (sizes[taker] == 0), 0, jnp.maximum(slack, 0))
    shifted = jax.random.randint(jax.random.fold_in(own, 4), (number_of // 2,), 0, 1 << 20) % (slack + 1)
    sizes = sizes.at[giver].add(-shifted).at[taker].add(shifted)
    labels = jnp.searchsorted(jnp.cumsum(sizes), jnp.arange(rows * top), side="right").astype(jnp.int32)
    grid = labels.reshape(top, rows).T
    grid = grid[jax.random.permutation(jax.random.fold_in(own, 1), rows)]
    turn = jax.random.randint(jax.random.fold_in(own, 2), (rows, 1), 0, top)
    return jnp.take_along_axis(grid, (jnp.arange(top)[None, :] + turn) % top, axis=1)


def portions_of(count, total, bound, skew, full):
    weights = [(1 << 20) // math.isqrt(rank ** skew) + 1 for rank in range(1, count + 1)]
    largest = bound if full else min(bound, max(-(-total // count), total * weights[0] // sum(weights)))
    least = 1 if total - largest >= count - 1 else 0
    counts, surplus = [largest] + [least] * (count - 1), total - largest - least * (count - 1)
    while surplus > 0:
        free = [i for i in range(1, count) if counts[i] < largest] or [i for i in range(1, count) if counts[i] < bound]
        pool, budget = sum([weights[i] for i in free]), surplus
        for i in free:
            extra = min(bound - counts[i], max(1, budget * weights[i] // pool), surplus)
            counts[i] = counts[i] + extra
            surplus = surplus - extra
    return np.array(counts)


def scatter_about(own_key, shape, width, most, split=(), kind=jnp.bfloat16):
    drawn = jax.random.normal(own_key, shape, jnp.float32) * width
    if len(split) > 0:
        drawn = steps_of(own_key, shape, split, -0.22, 0.18) * drawn
    return jnp.clip(drawn, min=-most, max=most).astype(kind)


def setup_inputs(seed: int = 0) -> dict:
    keys = jax.random.split(jax.random.key(seed), 9)
    grad_out = scatter_about(keys[0], (TOKENS, D), 1.0, 6.0, ((0, 128),))
    parked_inputs = scatter_about(keys[1], (2, TOKENS, HALF), 1.0, 6.0, ((0, 2), (1, 128)))
    route_ids_keys = jax.random.split(jax.random.fold_in(keys[2], 1), TOKENS // TOK)
    route_ids_turns = jax.random.permutation(jax.random.fold_in(keys[2], 3), TOKENS // TOK)
    route_ids = jax.vmap(lambda own, number: shared_out(jax.random.fold_in(keys[2], 2), own, number, TOK, EXPERTS, TOPK, CAP, 1))(route_ids_keys, route_ids_turns).reshape((TOKENS, TOPK))
    route_probs = jnp.clip(0.1 + 0.79999997 * jax.random.uniform(keys[3], (TOKENS, TOPK), jnp.float32) ** steps_of(keys[3], (TOKENS, TOPK), ((0, 128),), -0.2, 0.2), 0.1, 0.9)
    flight_expert = jax.random.randint(keys[4], (1,), 0, EXPERTS).astype(jnp.int32)
    w_gate = scatter_about(keys[5], (D, FF), D ** -0.5, 0.078125, ((1, 128),))
    w_up = scatter_about(keys[6], (D, FF), D ** -0.5, 0.078125, ((1, 128),))
    w_down = scatter_about(keys[7], (FF, D), FF ** -0.5, 0.0625, ((0, 128),))
    return dict(grad_out=grad_out, parked_inputs=parked_inputs, route_ids=route_ids, route_probs=route_probs, flight_expert=flight_expert, w_gate=w_gate, w_up=w_up, w_down=w_down)


def reference(grad_out, parked_inputs, route_ids, route_probs, flight_expert, w_gate, w_up, w_down):
    inputs = jnp.concatenate([parked_inputs[0], parked_inputs[1]], axis=1)
    hits = route_ids == flight_expert[0]
    weight = jnp.sum(jnp.where(hits, route_probs, jnp.float32(0.0)), axis=1)
    flags = jnp.any(hits, axis=1).astype(jnp.int32).reshape(N_EP, TOK)
    ranks = jnp.cumsum(flags, axis=1) - flags
    slot_ids = jnp.arange(CAP, dtype=jnp.int32)
    match = (ranks[:, None, :] == slot_ids[None, :, None]) & (flags[:, None, :] == 1)
    token_ids = jnp.arange(TOK, dtype=jnp.int32)
    slot_tok = jnp.sum(jnp.where(match, token_ids[None, None, :], 0), axis=2).astype(jnp.int32)
    valid = jnp.any(match, axis=2).reshape(-1, 1)
    row_index = (slot_tok + (jnp.arange(N_EP, dtype=jnp.int32) * TOK)[:, None]).reshape(-1)
    zero = jnp.zeros((), jnp.bfloat16)
    rows_x = jnp.where(valid, inputs[row_index], zero)
    rows_dy = jnp.where(valid, grad_out[row_index], zero)
    gate = jnp.dot(rows_x, w_gate, preferred_element_type=jnp.float32)
    up = jnp.dot(rows_x, w_up, preferred_element_type=jnp.float32)
    dhid = jnp.dot(rows_dy, w_down.T, preferred_element_type=jnp.float32)
    sig = jax.nn.sigmoid(gate)
    d_up = (dhid * gate * sig).astype(jnp.bfloat16)
    d_gate = (dhid * up * sig * (1.0 + gate * (1.0 - sig))).astype(jnp.bfloat16)
    rows_dx = jnp.dot(d_gate, w_gate.T, preferred_element_type=jnp.float32) + jnp.dot(d_up, w_up.T, preferred_element_type=jnp.float32)
    contrib = jnp.einsum("bct,bcd->btd", match.astype(jnp.float32), rows_dx.reshape(N_EP, CAP, -1), precision=lax.Precision.HIGHEST)
    contrib = contrib.reshape(N_EP * TOK, -1)
    total = grad_out.astype(jnp.float32) + 0.5 * weight[:, None] * contrib
    return total.astype(jnp.bfloat16)
```

```python
import jax
import jax.numpy as jnp
from jax import lax
from jax.experimental import pallas as pl
from jax.experimental.pallas import tpu as pltpu
from jax.sharding import PartitionSpec as P

MESH = pl.DeviceIdType.MESH
BF16 = jnp.bfloat16
F32 = jnp.float32

CAP = 34
TOK = 128
FFD = 64
NX, NY, NZ = 4, 4, 8
MAIN = 32
ROWS = 16 * CAP
TAIL0 = 16 * MAIN
PIECES = 8
NUM_SEMS = 112
NT_DIMS = (((1,), (1,)), ((), ()))
NN_DIMS = (((1,), (0,)), ((), ()))
TN_DIMS = (((0,), (0,)), ((), ()))


def dot(a, b, dims=NN_DIMS):
    return lax.dot_general(a, b, dims, preferred_element_type=F32)


def iota(shape, dim):
    return lax.broadcasted_iota(jnp.int32, shape, dim)


def kernel(half, fe, ids, probs, grad, parked, wg, wu, wd, out,
           gbuf, pbuf, rx, rdy, tx, tdy, w0, wp, wf, acc, ps, pr, dbuf,
           sa, sb, rta, rba, rla, rra, rtb, rbb, rlb, rrb,
           sa2, sb2, rta2, rba2, rla2, rra2, rtb2, rbb2, rlb2, rrb2,
           t2, rtt, rlt, rrt, send_sem, recv_sem, local_sem):
    piece = half // PIECES
    hc = half // 2
    core = lax.axis_index("swap")
    ep = lax.axis_index("ep")
    y = ep % NY
    z = (ep // NY) % NZ
    x = ep // (NY * NZ)

    def chip(dx, dy, dz):
        place = (((x + dx + NX) % NX) * NZ + (z + dz + NZ) % NZ) * NY + (y + dy + NY) % NY
        return (core, place)

    xp, xm = chip(1, 0, 0), chip(-1, 0, 0)
    yp, ym = chip(0, 1, 0), chip(0, -1, 0)
    zp, zm = chip(0, 0, 1), chip(0, 0, -1)
    other = (1 - core, ep)

    copies = []

    def send(src, dst, device):
        k = len(copies)
        copy = pltpu.make_async_remote_copy(
            src_ref=src, dst_ref=dst, send_sem=send_sem.at[k], recv_sem=recv_sem.at[k],
            device_id=device, device_id_type=MESH)
        copies.append(copy)
        copy.start()
        return copy

    cols = pl.ds(pl.multiple_of(core * half, half), half)
    local = [
        pltpu.make_async_copy(parked.at[0], pbuf, local_sem.at[0]),
        pltpu.make_async_copy(grad.at[:, cols], gbuf, local_sem.at[1]),
        pltpu.make_async_copy(wg.at[:, cols], w0.at[0], local_sem.at[2]),
        pltpu.make_async_copy(wu.at[:, cols], w0.at[1], local_sem.at[3]),
        pltpu.make_async_copy(wd.at[:, cols], w0.at[2], local_sem.at[4]),
    ]
    barrier = pltpu.get_barrier_semaphore()
    for peer in (xp, xm, yp, ym, zp, zm, other):
        pl.semaphore_signal(barrier, inc=1, device_id=peer, device_id_type=MESH)
    for copy in local:
        copy.start()

    hits = ids[...] == fe[0]
    weight = jnp.sum(jnp.where(hits, probs[...], 0.0), axis=0, keepdims=True)
    flags = jnp.max(hits.astype(F32), axis=0, keepdims=True)
    before = (iota((TOK, TOK), 0) < iota((TOK, TOK), 1)).astype(F32).astype(BF16)
    ranks = dot(jnp.broadcast_to(flags, (16, TOK)).astype(BF16), before)[0:1]

    def match_of(slot, extra=None):
        rank_is = jnp.broadcast_to(ranks, slot.shape) == slot.astype(F32)
        m = jnp.where(rank_is, jnp.broadcast_to(flags, slot.shape), 0.0)
        if extra is not None:
            m = jnp.where(extra, m, 0.0)
        return m

    match_main = match_of(iota((MAIN, TOK), 0))
    tail_row = iota((16, TOK), 0)
    tail_slot = MAIN + tail_row % 2
    match_tail = match_of(tail_slot)
    pick = [match_of(tail_slot, tail_row // 2 == p).astype(BF16) for p in range(PIECES)]
    main16 = match_main.astype(BF16)

    def choose(src, rows, tails):
        rows[0:MAIN, :] = dot(main16, src[...]).astype(BF16)
        t = dot(pick[0], src[:, 0:piece])
        for p in range(1, PIECES):
            t = t + dot(pick[p], src[:, p * piece:(p + 1) * piece])
        tails[0:16, :] = t.astype(BF16)

    local[0].wait()
    choose(pbuf, rx, tx)
    local[1].wait()
    choose(gbuf, rdy, tdy)
    for copy in local[2:]:
        copy.wait()
    pl.semaphore_wait(barrier, 7)

    def rows_of(s, n=1):
        return pl.ds(MAIN * s, MAIN * n)

    def tails_of(s, n=1):
        return pl.ds(16 * s, 16 * n)

    px = [send(rx.at[rows_of(0)], rx.at[rows_of(3)], xp),
          send(rx.at[rows_of(0)], rx.at[rows_of(1)], xm),
          send(tx.at[tails_of(0)], tx.at[tails_of(3)], xp),
          send(tx.at[tails_of(0)], tx.at[tails_of(1)], xm)]
    pd = [send(rdy.at[rows_of(0)], rdy.at[rows_of(12)], yp),
          send(rdy.at[rows_of(0)], rdy.at[rows_of(4)], ym),
          send(tdy.at[tails_of(0)], tdy.at[tails_of(12)], yp),
          send(tdy.at[tails_of(0)], tdy.at[tails_of(4)], ym)]

    gu, dn = pl.ds(0, 2), pl.ds(2, 1)

    def ring(source, g, part, side):
        return send(source, wp.at[g, part, side], zp if side == 0 else zm)

    arrived = {}
    for part, name in ((gu, "gu"), (dn, "dn")):
        for side in (0, 1):
            arrived[0, name, side] = ring(w0.at[part], 0, part, side)

    def forward_rows(first, rows, tails, s3, s1, s2, plus, minus):
        for copy in first:
            copy.wait_recv()
        return [send(rows.at[pl.ds(MAIN * s3, 16)], rows.at[pl.ds(MAIN * s2, 16)], plus),
                send(rows.at[pl.ds(MAIN * s1 + 16, 16)], rows.at[pl.ds(MAIN * s2 + 16, 16)], minus),
                send(tails.at[tails_of(s1)], tails.at[tails_of(s2)], minus)]

    fx = forward_rows(px, rx, tx, 3, 1, 2, xp, xm)
    fd = forward_rows(pd, rdy, tdy, 12, 4, 8, yp, ym)
    for copy in fx:
        copy.wait_recv()
    px = [send(rx.at[rows_of(0, 4)], rx.at[rows_of(12, 4)], yp),
          send(rx.at[rows_of(0, 4)], rx.at[rows_of(4, 4)], ym),
          send(tx.at[tails_of(0, 4)], tx.at[tails_of(12, 4)], yp),
          send(tx.at[tails_of(0, 4)], tx.at[tails_of(4, 4)], ym)]
    for copy in fd:
        copy.wait_recv()
    pd_plus, pd_minus = [], []
    for j in range(4):
        pd_plus.append((send(rdy.at[rows_of(4 * j)], rdy.at[rows_of(4 * j + 3)], xp),
                        send(tdy.at[tails_of(4 * j)], tdy.at[tails_of(4 * j + 3)], xp)))
        pd_minus.append((send(rdy.at[rows_of(4 * j)], rdy.at[rows_of(4 * j + 1)], xm),
                         send(tdy.at[tails_of(4 * j)], tdy.at[tails_of(4 * j + 1)], xm)))

    def forward_weights(g, name, part):
        for side in (0, 1):
            arrived[g - 1, name, side].wait_recv()
            arrived[g, name, side] = ring(wp.at[g - 1, part, side], g, part, side)

    forward_weights(1, "gu", gu)

    for copy in px:
        copy.wait_recv()
    last = [send(rx.at[rows_of(12, 2)], rx.at[rows_of(8, 2)], yp),
            send(rx.at[rows_of(6, 2)], rx.at[rows_of(10, 2)], ym),
            send(tx.at[tails_of(12, 2)], tx.at[tails_of(8, 2)], yp),
            send(tx.at[tails_of(6, 2)], tx.at[tails_of(10, 2)], ym)]
    for pair in pd_plus + pd_minus:
        for copy in pair:
            copy.wait_recv()
    for j in range(4):
        s, to = (4 * j + 3, xp) if j < 2 else (4 * j + 1, xm)
        last.append(send(rdy.at[rows_of(s)], rdy.at[rows_of(4 * j + 2)], to))
        last.append(send(tdy.at[tails_of(s)], tdy.at[tails_of(4 * j + 2)], to))
    forward_weights(1, "dn", dn)
    for copy in last:
        copy.wait_recv()

    row, col = iota((MAIN, 256), 0), iota((MAIN, 256), 1)
    block = row // 2
    base = 16 * (4 * (block % 4) + block // 4) + row % 2
    for p in range(PIECES):
        e = jnp.where(col == base + 2 * p, 1.0, 0.0).astype(BF16)
        for tails, rows in ((tx, rx), (tdy, rdy)):
            rows[TAIL0:ROWS, p * piece:(p + 1) * piece] = dot(e, tails[...]).astype(BF16)

    def weights_of(g):
        if g == 0 or g == 4:
            w = w0 if g == 0 else wf
            return w[0:2].reshape(2 * FFD, half), w[2]
        return wp[g - 1, 0:2].reshape(4 * FFD, half), wp[g - 1, 2].reshape(2 * FFD, half)

    def width_of(g):
        return FFD if g in (0, 4) else 2 * FFD

    def partial_gate(g):
        wgu, _ = weights_of(g)

        @pl.loop(0, 2)
        def _(m):
            rows = pl.ds(pl.multiple_of(m * (ROWS // 2), 16), ROWS // 2)
            ps[g, rows, 0:2 * width_of(g)] = dot(rx[rows, :], wgu, NT_DIMS)

    def partial_dhid(g):
        _, wdn = weights_of(g)
        width = width_of(g)

        @pl.loop(0, 2)
        def _(m):
            rows = pl.ds(pl.multiple_of(m * (ROWS // 2), 16), ROWS // 2)
            dh = dot(rdy[rows, :], wdn, NT_DIMS)
            if width == FFD:
                dh = jnp.concatenate([dh, jnp.zeros_like(dh)], axis=1)
            ps[g, rows, 2 * width:2 * width + 128] = dh

    def exchange(g):
        used = pl.ds(0, 2 * width_of(g) + 128)
        return send(ps.at[g, :, used], pr.at[g, :, used], other)

    def finish(g, copy):
        copy.wait_recv()
        width = width_of(g)

        @pl.loop(0, ROWS // 32)
        def _(m):
            rows = pl.ds(pl.multiple_of(m * 32, 32), 32)
            total = ps[g, rows, 0:2 * width + 128] + pr[g, rows, 0:2 * width + 128]
            gate, up = total[:, 0:width], total[:, width:2 * width]
            dhid = total[:, 2 * width:3 * width]
            s = 1.0 / (1.0 + jnp.exp(-gate))
            d_up = dhid * gate * s
            d_gate = dhid * up * s * (1.0 + gate * (1.0 - s))
            dbuf[rows, 0:2 * width] = jnp.concatenate([d_gate, d_up], axis=1).astype(BF16)

    tile = 512

    def back_tiles(g, lo, hi):
        width = width_of(g)

        @pl.loop(lo // tile, hi // tile)
        def _(n):
            at = pl.ds(pl.multiple_of(n * tile, tile), tile)
            if g == 0 or g == 4:
                w = (w0 if g == 0 else wf)[0:2, :, at].reshape(2 * FFD, tile)
            else:
                w = wp[g - 1, 0:2, :, :, at].reshape(4 * FFD, tile)
            value = dot(dbuf[:, 0:2 * width], w)
            if g == 0:
                acc[:, at] = value
            else:
                acc[:, at] += value

    def group(g):
        partial_gate(g)
        partial_dhid(g)
        copy = exchange(g)
        finish(g, copy)
        back_tiles(g, 0, half)

    group(0)
    group(1)
    forward_weights(2, "gu", gu)
    forward_weights(2, "dn", dn)
    group(2)

    def forward_far(name, part):
        result = []
        for side in (0, 1):
            arrived[2, name, side].wait_recv()
            hid = pl.ds(32 * side, 32)
            result.append(send(wp.at[2, part, side, hid], wf.at[part, hid], zp if side == 0 else zm))
        return result

    far_gu = forward_far("gu", gu)
    partial_gate(3)
    far_dn = forward_far("dn", dn)
    partial_dhid(3)
    copy = exchange(3)
    finish(3, copy)
    back_tiles(3, 0, half)
    for copy in far_gu:
        copy.wait_recv()
    partial_gate(4)
    for copy in far_dn:
        copy.wait_recv()
    partial_dhid(4)
    copy = exchange(4)
    finish(4, copy)

    def add(a, b):
        return (a.astype(F32) + b.astype(F32)).astype(BF16)

    def start_ring(unit, h, top, bottom, left, right, plus, minus):
        size = unit.shape[1]
        up, down = pl.ds(0, h), pl.ds(h, size - h)
        return [send(unit.at[2, up], top, plus), send(unit.at[2, down], bottom, minus),
                send(unit.at[1, down], left.at[down], plus), send(unit.at[3, up], right.at[up], minus)]

    def turn_ring(begun, unit, h, top, bottom, left, right, plus, minus):
        size = unit.shape[1]
        up, down = pl.ds(0, h), pl.ds(h, size - h)
        begun[0].wait_recv()
        unit[1, up] = add(unit[1, up], top[...])
        ends = [begun[2], begun[3], send(unit.at[1, up], left.at[up], plus)]
        begun[1].wait_recv()
        unit[3, down] = add(unit[3, down], bottom[...])
        ends.append(send(unit.at[3, down], right.at[down], minus))
        return ends

    back_tiles(4, hc, half)
    for j in (2, 1, 3, 0):
        sb[j] = acc[128 * j:128 * j + 128, hc:half].astype(BF16)
    ring_b = (sb, 64, rtb, rbb, rlb, rrb, yp, ym)
    begun_b = start_ring(*ring_b)
    back_tiles(4, 0, hc)
    for i in (2, 1, 3, 0):
        for j in range(4):
            s = 4 * j + i
            sa[i, 32 * j:32 * j + 32] = acc[MAIN * s:MAIN * s + MAIN, 0:hc].astype(BF16)
        t = acc[TAIL0 + 8 * i:TAIL0 + 8 * i + 8, :]
        sa[i, 128:144] = jnp.concatenate([t[:, 0:hc], t[:, hc:half]], axis=0).astype(BF16)
    ring_a = (sa, 64, rta, rba, rla, rra, xp, xm)
    begun_a = start_ring(*ring_a)
    ends_b = turn_ring(begun_b, *ring_b)
    ends_a = turn_ring(begun_a, *ring_a)

    for copy in ends_b:
        copy.wait_recv()
    for i in range(4):
        rows = slice(32 * i, 32 * i + 32)
        sb2[i] = (sb[0, rows].astype(F32) + rlb[rows].astype(F32) + rrb[rows].astype(F32)).astype(BF16)
    ring_b2 = (sb2, 16, rtb2, rbb2, rlb2, rrb2, xp, xm)
    begun_b2 = start_ring(*ring_b2)
    for copy in ends_a:
        copy.wait_recv()
    for j in range(4):
        rows = slice(32 * j, 32 * j + 32)
        sa2[j] = (sa[0, rows].astype(F32) + rla[rows].astype(F32) + rra[rows].astype(F32)).astype(BF16)
    ring_a2 = (sa2, 16, rta2, rba2, rla2, rra2, yp, ym)
    begun_a2 = start_ring(*ring_a2)
    tail = (sa[0, 128:144].astype(F32) + rla[128:144].astype(F32) + rra[128:144].astype(F32)).astype(BF16)
    row, col = iota((64, 16), 0), iota((64, 16), 1)
    p_of = (row % 16) // 2
    wanted = 8 * (p_of // 4) + 2 * (row // 16) + row % 2
    packed = jnp.zeros((64, piece), F32)
    for q in range(4):
        f = jnp.where((col == wanted) & (p_of % 4 == q), 1.0, 0.0).astype(BF16)
        packed = packed + dot(f, tail[:, q * piece:(q + 1) * piece])
    t2[...] = packed.astype(BF16).reshape(4, 16, piece)
    tail_far = send(t2.at[2], rtt, yp)
    tail_right = send(t2.at[3], rrt, ym)
    ends_b2 = turn_ring(begun_b2, *ring_b2)
    ends_a2 = turn_ring(begun_a2, *ring_a2)
    tail_far.wait_recv()
    t2[1] = add(t2[1], rtt[...])
    tail_left = send(t2.at[1], rlt, yp)

    slot_weight = 0.5 * jnp.sum(match_main * weight, axis=1, keepdims=True)
    tail_weight = 0.5 * jnp.sum(match_tail * weight, axis=1, keepdims=True)
    for copy in ends_b2 + ends_a2 + [tail_right, tail_left]:
        copy.wait_recv()
    tail = (t2[0].astype(F32) + rlt[...].astype(F32) + rrt[...].astype(F32)) * tail_weight
    for p in range(PIECES):
        at = slice(p * piece, (p + 1) * piece)
        own, left, right = (sa2, rla2, rra2) if p < 4 else (sb2, rlb2, rrb2)
        q = slice((p % 4) * piece, (p % 4 + 1) * piece)
        main = (own[0, :, q].astype(F32) + left[:, q].astype(F32) + right[:, q].astype(F32)) * slot_weight
        value = jnp.concatenate([main, tail], axis=0)
        high = value.astype(BF16)
        low = (value - high.astype(F32)).astype(BF16)
        m = jnp.concatenate([main16, pick[p]], axis=0)
        spread = dot(m, high, TN_DIMS) + dot(m, low, TN_DIMS)
        out[:, at] = (gbuf[:, at].astype(F32) + spread).astype(BF16)

    for copy in copies:
        copy.wait_send()


def solution(mesh):
    def on_device(grad_out, parked_inputs, route_ids, route_probs, flight_expert, w_gate, w_up, w_down):
        features = grad_out.shape[1]
        half = features // 2
        hc = half // 2
        piece = half // PIECES
        vmem = pltpu.VMEM
        scratch = [
            vmem((TOK, half), BF16), vmem((TOK, half), BF16),
            vmem((ROWS, half), BF16), vmem((ROWS, half), BF16),
            vmem((256, piece), BF16), vmem((256, piece), BF16),
            vmem((3, FFD, half), BF16), vmem((3, 3, 2, FFD, half), BF16), vmem((3, FFD, half), BF16),
            vmem((ROWS, half), F32),
            vmem((5, ROWS, 384), F32), vmem((5, ROWS, 384), F32),
            vmem((ROWS, 256), BF16),
            vmem((4, 144, hc), BF16), vmem((4, 128, hc), BF16),
            vmem((64, hc), BF16), vmem((80, hc), BF16), vmem((144, hc), BF16), vmem((144, hc), BF16),
            vmem((64, hc), BF16), vmem((64, hc), BF16), vmem((128, hc), BF16), vmem((128, hc), BF16),
            vmem((4, 32, hc), BF16), vmem((4, 32, hc), BF16),
            vmem((16, hc), BF16), vmem((16, hc), BF16), vmem((32, hc), BF16), vmem((32, hc), BF16),
            vmem((16, hc), BF16), vmem((16, hc), BF16), vmem((32, hc), BF16), vmem((32, hc), BF16),
            vmem((4, 16, piece), BF16),
            vmem((16, piece), BF16), vmem((16, piece), BF16), vmem((16, piece), BF16),
            pltpu.SemaphoreType.DMA((NUM_SEMS,)), pltpu.SemaphoreType.DMA((NUM_SEMS,)),
            pltpu.SemaphoreType.DMA((5,)),
        ]
        any_space = pl.BlockSpec(memory_space=pl.ANY)
        in_vmem = pl.BlockSpec(memory_space=pltpu.VMEM)

        def body(*refs):
            kernel(half, *refs)

        return pl.pallas_call(
            body,
            out_shape=jax.ShapeDtypeStruct((TOK, half), BF16),
            in_specs=[pl.BlockSpec(memory_space=pltpu.SMEM), in_vmem, in_vmem,
                      any_space, any_space, any_space, any_space, any_space],
            out_specs=in_vmem,
            scratch_shapes=scratch,
            compiler_params=pltpu.CompilerParams(
                collective_id=0, has_side_effects=True, vmem_limit_bytes=60 * 1024 * 1024),
            cost_estimate=pl.CostEstimate(
                flops=10 * ROWS * 8 * FFD * half, bytes_accessed=10_000_000, transcendentals=ROWS * 512),
            name="routed_swiglu_backward",
        )(flight_expert, route_ids.T, route_probs.T, grad_out, parked_inputs, w_gate.T, w_up.T, w_down)

    in_specs = (
        P("ep", None),
        P("swap", "ep", None),
        P("ep", None),
        P("ep", None),
        P(),
        P(None, "ep"),
        P(None, "ep"),
        P("ep", None),
    )
    return jax.shard_map(
        on_device, mesh=mesh, in_specs=in_specs, out_specs=P("ep", "swap"), check_vma=False
    )
```

```python
import jax
import jax.numpy as jnp
from jax import lax
from jax.experimental import pallas as pl
from jax.experimental.pallas import tpu as pltpu
from jax.sharding import PartitionSpec as P

MESH = pl.DeviceIdType.MESH
BF16 = jnp.bfloat16
F32 = jnp.float32

CAP = 34
TOK = 128
FFD = 64
NX, NY, NZ = 4, 4, 8
MAIN = 32
ROWS = 16 * CAP
TAIL0 = 16 * MAIN
PIECES = 8
NUM_SEMS = 128
NT_DIMS = (((1,), (1,)), ((), ()))
NN_DIMS = (((1,), (0,)), ((), ()))
TN_DIMS = (((0,), (0,)), ((), ()))


def dot(a, b, dims=NN_DIMS):
    return lax.dot_general(a, b, dims, preferred_element_type=F32)


def iota(shape, dim):
    return lax.broadcasted_iota(jnp.int32, shape, dim)


def kernel(half, fe, ids, probs, grad, parked, wg, wu, wd, out,
           gbuf, pbuf, rx, rdy, tx, tdy, w0, wp, wf, acc, ps, pr, dbuf,
           sa_0, rta_0, rba_0, rla_0, rra_0, sa_1, rta_1, rba_1, rla_1, rra_1,
           sb_0, rtb_0, rbb_0, rlb_0, rrb_0, sb_1, rtb_1, rbb_1, rlb_1, rrb_1,
           sa2_0, ra2_0, sa2_1, ra2_1, sb2_0, rb2_0, sb2_1, rb2_1,
           t1, t1r, t2, t2r, send_sem, recv_sem, local_sem):
    piece = half // PIECES
    hc = half // 2
    core = lax.axis_index("swap")
    ep = lax.axis_index("ep")
    y = ep % NY
    z = (ep // NY) % NZ
    x = ep // (NY * NZ)

    def chip(dx, dy, dz):
        place = (((x + dx + NX) % NX) * NZ + (z + dz + NZ) % NZ) * NY + (y + dy + NY) % NY
        return (core, place)

    xp, xm = chip(1, 0, 0), chip(-1, 0, 0)
    yp, ym = chip(0, 1, 0), chip(0, -1, 0)
    zp, zm = chip(0, 0, 1), chip(0, 0, -1)
    xf, yf = chip(2, 0, 0), chip(0, 2, 0)
    a_refs = [(sa_0, rta_0, rba_0, rla_0, rra_0), (sa_1, rta_1, rba_1, rla_1, rra_1)]
    b_refs = [(sb_0, rtb_0, rbb_0, rlb_0, rrb_0), (sb_1, rtb_1, rbb_1, rlb_1, rrb_1)]
    sa2, ra2, sb2, rb2 = (sa2_0, sa2_1), (ra2_0, ra2_1), (sb2_0, sb2_1), (rb2_0, rb2_1)
    other = (1 - core, ep)

    copies = []

    def send(src, dst, device):
        k = len(copies)
        copy = pltpu.make_async_remote_copy(
            src_ref=src, dst_ref=dst, send_sem=send_sem.at[k], recv_sem=recv_sem.at[k],
            device_id=device, device_id_type=MESH)
        copies.append(copy)
        copy.start()
        return copy

    cols = pl.ds(pl.multiple_of(core * half, half), half)
    local = [
        pltpu.make_async_copy(parked.at[0], pbuf, local_sem.at[0]),
        pltpu.make_async_copy(grad.at[:, cols], gbuf, local_sem.at[1]),
        pltpu.make_async_copy(wg.at[:, cols], w0.at[0], local_sem.at[2]),
        pltpu.make_async_copy(wu.at[:, cols], w0.at[1], local_sem.at[3]),
        pltpu.make_async_copy(wd.at[:, cols], w0.at[2], local_sem.at[4]),
    ]
    barrier = pltpu.get_barrier_semaphore()
    for peer in (xp, xm, yp, ym, zp, zm, xf, yf, other):
        pl.semaphore_signal(barrier, inc=1, device_id=peer, device_id_type=MESH)
    for copy in local[2:] + local[:2]:
        copy.start()

    hits = ids[...] == fe[0]
    weight = jnp.sum(jnp.where(hits, probs[...], 0.0), axis=0, keepdims=True)
    flags = jnp.max(hits.astype(F32), axis=0, keepdims=True)
    before = (iota((TOK, TOK), 0) < iota((TOK, TOK), 1)).astype(F32).astype(BF16)
    ranks = dot(jnp.broadcast_to(flags, (16, TOK)).astype(BF16), before)[0:1]

    def match_of(slot, extra=None):
        rank_is = jnp.broadcast_to(ranks, slot.shape) == slot.astype(F32)
        m = jnp.where(rank_is, jnp.broadcast_to(flags, slot.shape), 0.0)
        if extra is not None:
            m = jnp.where(extra, m, 0.0)
        return m

    match_main = match_of(iota((MAIN, TOK), 0))
    tail_row = iota((16, TOK), 0)
    tail_slot = MAIN + tail_row % 2
    match_tail = match_of(tail_slot)
    pick = [match_of(tail_slot, tail_row // 2 == p).astype(BF16) for p in range(PIECES)]
    main16 = match_main.astype(BF16)

    def choose(src, rows, tails):
        rows[0:MAIN, :] = dot(main16, src[...]).astype(BF16)
        t = dot(pick[0], src[:, 0:piece])
        for p in range(1, PIECES):
            t = t + dot(pick[p], src[:, p * piece:(p + 1) * piece])
        tails[0:16, :] = t.astype(BF16)

    for copy in local[2:]:
        copy.wait()
    pl.semaphore_wait(barrier, 9)

    gu, dn = pl.ds(0, 2), pl.ds(2, 1)

    def ring(source, g, part, side):
        return send(source, wp.at[g, part, side], zp if side == 0 else zm)

    arrived = {}
    for part, name in ((gu, "gu"), (dn, "dn")):
        for side in (0, 1):
            arrived[0, name, side] = ring(w0.at[part], 0, part, side)

    def rows_of(s, n=1):
        return pl.ds(MAIN * s, MAIN * n)

    def tails_of(s, n=1):
        return pl.ds(16 * s, 16 * n)

    local[0].wait()
    choose(pbuf, rx, tx)
    px = [send(rx.at[rows_of(0)], rx.at[rows_of(3)], xp),
          send(rx.at[rows_of(0)], rx.at[rows_of(1)], xm),
          send(tx.at[tails_of(0)], tx.at[tails_of(3)], xp),
          send(tx.at[tails_of(0)], tx.at[tails_of(1)], xm)]
    local[1].wait()
    choose(gbuf, rdy, tdy)
    pd = [send(rdy.at[rows_of(0)], rdy.at[rows_of(12)], yp),
          send(rdy.at[rows_of(0)], rdy.at[rows_of(4)], ym),
          send(tdy.at[tails_of(0)], tdy.at[tails_of(12)], yp),
          send(tdy.at[tails_of(0)], tdy.at[tails_of(4)], ym)]

    def forward_rows(first, rows, tails, s3, s1, s2, plus, minus):
        for copy in first:
            copy.wait_recv()
        return [send(rows.at[pl.ds(MAIN * s3, 16)], rows.at[pl.ds(MAIN * s2, 16)], plus),
                send(rows.at[pl.ds(MAIN * s1 + 16, 16)], rows.at[pl.ds(MAIN * s2 + 16, 16)], minus),
                send(tails.at[tails_of(s1)], tails.at[tails_of(s2)], minus)]

    fx = forward_rows(px, rx, tx, 3, 1, 2, xp, xm)
    fd = forward_rows(pd, rdy, tdy, 12, 4, 8, yp, ym)
    for copy in fx:
        copy.wait_recv()
    px = [send(rx.at[rows_of(0, 4)], rx.at[rows_of(12, 4)], yp),
          send(rx.at[rows_of(0, 4)], rx.at[rows_of(4, 4)], ym),
          send(tx.at[tails_of(0, 4)], tx.at[tails_of(12, 4)], yp),
          send(tx.at[tails_of(0, 4)], tx.at[tails_of(4, 4)], ym)]
    for copy in fd:
        copy.wait_recv()
    pd_plus, pd_minus = [], []
    for j in range(4):
        pd_plus.append((send(rdy.at[rows_of(4 * j)], rdy.at[rows_of(4 * j + 3)], xp),
                        send(tdy.at[tails_of(4 * j)], tdy.at[tails_of(4 * j + 3)], xp)))
        pd_minus.append((send(rdy.at[rows_of(4 * j)], rdy.at[rows_of(4 * j + 1)], xm),
                         send(tdy.at[tails_of(4 * j)], tdy.at[tails_of(4 * j + 1)], xm)))

    def forward_weights(g, name, part):
        for side in (0, 1):
            arrived[g - 1, name, side].wait_recv()
            arrived[g, name, side] = ring(wp.at[g - 1, part, side], g, part, side)

    forward_weights(1, "gu", gu)

    for copy in px:
        copy.wait_recv()
    last = [send(rx.at[rows_of(12, 2)], rx.at[rows_of(8, 2)], yp),
            send(rx.at[rows_of(6, 2)], rx.at[rows_of(10, 2)], ym),
            send(tx.at[tails_of(12, 2)], tx.at[tails_of(8, 2)], yp),
            send(tx.at[tails_of(6, 2)], tx.at[tails_of(10, 2)], ym)]
    for pair in pd_plus + pd_minus:
        for copy in pair:
            copy.wait_recv()
    for j in range(4):
        s, to = (4 * j + 3, xp) if j < 2 else (4 * j + 1, xm)
        last.append(send(rdy.at[rows_of(s)], rdy.at[rows_of(4 * j + 2)], to))
        last.append(send(tdy.at[tails_of(s)], tdy.at[tails_of(4 * j + 2)], to))
    forward_weights(1, "dn", dn)
    for copy in last:
        copy.wait_recv()

    row, col = iota((MAIN, 256), 0), iota((MAIN, 256), 1)
    block = row // 2
    base = 16 * (4 * (block % 4) + block // 4) + row % 2
    for p in range(PIECES):
        e = jnp.where(col == base + 2 * p, 1.0, 0.0).astype(BF16)
        for tails, rows in ((tx, rx), (tdy, rdy)):
            rows[TAIL0:ROWS, p * piece:(p + 1) * piece] = dot(e, tails[...]).astype(BF16)

    def weights_of(g):
        if g == 0 or g == 4:
            w = w0 if g == 0 else wf
            return w[0:2].reshape(2 * FFD, half), w[2]
        return wp[g - 1, 0:2].reshape(4 * FFD, half), wp[g - 1, 2].reshape(2 * FFD, half)

    def width_of(g):
        return FFD if g in (0, 4) else 2 * FFD

    def partial_gate(g):
        wgu, _ = weights_of(g)

        @pl.loop(0, 2)
        def _(m):
            rows = pl.ds(pl.multiple_of(m * (ROWS // 2), 16), ROWS // 2)
            ps[g, rows, 0:2 * width_of(g)] = dot(rx[rows, :], wgu, NT_DIMS)

    def partial_dhid(g):
        _, wdn = weights_of(g)
        width = width_of(g)

        @pl.loop(0, 2)
        def _(m):
            rows = pl.ds(pl.multiple_of(m * (ROWS // 2), 16), ROWS // 2)
            dh = dot(rdy[rows, :], wdn, NT_DIMS)
            if width == FFD:
                dh = jnp.concatenate([dh, jnp.zeros_like(dh)], axis=1)
            ps[g, rows, 2 * width:2 * width + 128] = dh

    def exchange(g):
        used = pl.ds(0, 2 * width_of(g) + 128)
        return send(ps.at[g, :, used], pr.at[g, :, used], other)

    def finish(g, begun, lo=0, hi=ROWS // 32):
        for copy in begun:
            copy.wait_recv()
        width = width_of(g)

        @pl.loop(lo, hi)
        def _(m):
            rows = pl.ds(pl.multiple_of(m * 32, 32), 32)
            total = ps[g, rows, 0:2 * width + 128] + pr[g, rows, 0:2 * width + 128]
            gate, up = total[:, 0:width], total[:, width:2 * width]
            dhid = total[:, 2 * width:3 * width]
            s = 1.0 / (1.0 + jnp.exp(-gate))
            d_up = dhid * gate * s
            d_gate = dhid * up * s * (1.0 + gate * (1.0 - s))
            dbuf[rows, 0:2 * width] = jnp.concatenate([d_gate, d_up], axis=1).astype(BF16)

    tile = half // 6

    def back_tiles(g):
        width = width_of(g)

        @pl.loop(0, half // tile)
        def _(n):
            at = pl.ds(pl.multiple_of(n * tile, tile), tile)
            if g == 0:
                w = w0[0:2, :, at].reshape(2 * FFD, tile)
            else:
                w = wp[g - 1, 0:2, :, :, at].reshape(4 * FFD, tile)
            value = dot(dbuf[:, 0:2 * width], w)
            if g == 0:
                acc[:, at] = value
            else:
                acc[:, at] += value

    def begin(g):
        partial_gate(g)
        partial_dhid(g)
        return exchange(g)

    begun0, begun1 = begin(0), begin(1)
    forward_weights(2, "gu", gu)
    finish(0, [begun0])
    back_tiles(0)
    finish(1, [begun1])
    back_tiles(1)
    forward_weights(2, "dn", dn)
    begun2 = begin(2)
    finish(2, [begun2])
    back_tiles(2)

    def forward_far(name, part):
        result = []
        for side in (0, 1):
            arrived[2, name, side].wait_recv()
            hid = pl.ds(32 * side, 32)
            result.append(send(wp.at[2, part, side, hid], wf.at[part, hid], zp if side == 0 else zm))
        return result

    far_gu = forward_far("gu", gu)
    partial_gate(3)
    far_dn = forward_far("dn", dn)
    partial_dhid(3)
    finish(3, [exchange(3)])
    back_tiles(3)
    for copy in far_gu:
        copy.wait_recv()
    partial_gate(4)
    far_gate = send(ps.at[4, :, pl.ds(0, 128)], pr.at[4, :, pl.ds(0, 128)], other)
    for copy in far_dn:
        copy.wait_recv()
    far_dhid = []
    for first, count in ((0, 288), (288, 256)):
        dh = dot(rdy[first:first + count, :], wf[2], NT_DIMS)
        ps[4, first:first + count, 128:256] = jnp.concatenate([dh, jnp.zeros_like(dh)], axis=1)
        at = (4, pl.ds(first, count), pl.ds(128, 128))
        far_dhid.append(send(ps.at[at], pr.at[at], other))
    finish(4, [far_gate, far_dhid[0]], 0, 9)
    finish(4, [far_dhid[1]], 9, 17)

    def add(a, b):
        return (a.astype(F32) + b.astype(F32)).astype(BF16)

    def start_ring(ring):
        unit, top, bottom, left, right, plus, minus = ring
        up, down = pl.ds(0, 64), pl.ds(64, 64)
        return [send(unit.at[2, up], top, plus), send(unit.at[2, down], bottom, minus)]

    def rest_ring(ring):
        unit, top, bottom, left, right, plus, minus = ring
        up, down = pl.ds(0, 64), pl.ds(64, 64)
        return [send(unit.at[1, down], left.at[down], plus), send(unit.at[3, up], right.at[up], minus)]

    def turn_ring(begun, ends, ring):
        unit, top, bottom, left, right, plus, minus = ring
        up, down = pl.ds(0, 64), pl.ds(64, 64)
        begun[0].wait_recv()
        unit[1, up] = add(unit[1, up], top[...])
        ends.append(send(unit.at[1, up], left.at[up], plus))
        begun[1].wait_recv()
        unit[3, down] = add(unit[3, down], bottom[...])
        ends.append(send(unit.at[3, down], right.at[down], minus))

    def second(ends, ring, unit, arrivals, plus, minus, far):
        own, _, _, left, right, _, _ = ring
        for copy in ends:
            copy.wait_recv()
        for k in (2, 1, 3, 0):
            rows = slice(32 * k, 32 * k + 32)
            unit[k] = (own[0, rows].astype(F32) + left[rows].astype(F32) + right[rows].astype(F32)).astype(BF16)
        return scatter(unit, arrivals, plus, minus, far)

    def scatter(unit, arrivals, plus, minus, far):
        return [send(unit.at[2], arrivals.at[1], far),
                send(unit.at[1], arrivals.at[0], plus), send(unit.at[3], arrivals.at[2], minus)]

    rings_a = [a + (xp, xm) for a in a_refs]
    rings_b = [b + (yp, ym) for b in b_refs]

    def last_tiles(c, is_a):
        n0, n1 = (0, 3) if c == 0 else (3, 4)
        for n in range(n0, n1):
            p = n if is_a else n + 4
            at = slice(p * piece, (p + 1) * piece)
            to = slice((n - n0) * piece, (n - n0 + 1) * piece)
            value = acc[:, at] + dot(dbuf[:, 0:2 * FFD], wf[0:2, :, at].reshape(2 * FFD, piece))
            for i in range(4):
                for j in range(4):
                    s = 4 * j + i
                    block = value[MAIN * s:MAIN * s + MAIN].astype(BF16)
                    if is_a:
                        rings_a[c][0][i, 32 * j:32 * j + 32, to] = block
                    else:
                        rings_b[c][0][j, 32 * i:32 * i + 32, to] = block
            acc[TAIL0:ROWS, at] = value[TAIL0:ROWS]

    begun_a, begun_b, ends_a, ends_b = [], [], [], []
    for c in range(2):
        last_tiles(c, False)
        begun_b.append(start_ring(rings_b[c]))
        last_tiles(c, True)
        begun_a.append(start_ring(rings_a[c]))
    for i in range(4):
        t = acc[TAIL0 + 8 * i:TAIL0 + 8 * i + 8, :]
        t1[i] = jnp.concatenate([t[:, 0:hc], t[:, hc:half]], axis=0).astype(BF16)
    tail_ends = scatter(t1, t1r, xp, xm, xf)
    for c in range(2):
        ends_b.append(rest_ring(rings_b[c]))
        ends_a.append(rest_ring(rings_a[c]))
        turn_ring(begun_b[c], ends_b[c], rings_b[c])
        turn_ring(begun_a[c], ends_a[c], rings_a[c])

    for copy in tail_ends:
        copy.wait_recv()
    tail = t1[0].astype(F32)
    for k in range(3):
        tail = tail + t1r[k].astype(F32)
    tail = tail.astype(BF16)
    row, col = iota((64, 16), 0), iota((64, 16), 1)
    p_of = (row % 16) // 2
    wanted = 8 * (p_of // 4) + 2 * (row // 16) + row % 2
    packed = jnp.zeros((64, piece), F32)
    for q in range(4):
        f = jnp.where((col == wanted) & (p_of % 4 == q), 1.0, 0.0).astype(BF16)
        packed = packed + dot(f, tail[:, q * piece:(q + 1) * piece])
    t2[...] = packed.astype(BF16).reshape(4, 16, piece)
    tail_ends = scatter(t2, t2r, yp, ym, yf)

    last_b, last_a = [], []
    for c in range(2):
        last_b.append(second(ends_b[c], rings_b[c], sb2[c], rb2[c], xp, xm, xf))
        last_a.append(second(ends_a[c], rings_a[c], sa2[c], ra2[c], yp, ym, yf))

    slot_weight = 0.5 * jnp.sum(match_main * weight, axis=1, keepdims=True)
    tail_weight = 0.5 * jnp.sum(match_tail * weight, axis=1, keepdims=True)

    def total(unit, arrivals, at=None):
        if at is None:
            return unit[0].astype(F32) + arrivals[0].astype(F32) + arrivals[1].astype(F32) + arrivals[2].astype(F32)
        return (unit[0, :, at].astype(F32) + arrivals[0, :, at].astype(F32)
                + arrivals[1, :, at].astype(F32) + arrivals[2, :, at].astype(F32))

    for copy in tail_ends:
        copy.wait_recv()
    tail = total(t2, t2r) * tail_weight
    for c in range(2):
        for ends, unit, arrivals, p0 in ((last_b[c], sb2[c], rb2[c], 4), (last_a[c], sa2[c], ra2[c], 0)):
            for copy in ends:
                copy.wait_recv()
            n0, n1 = (0, 3) if c == 0 else (3, 4)
            for n in range(n0, n1):
                p = p0 + n
                at = slice(p * piece, (p + 1) * piece)
                q = slice((n - n0) * piece, (n - n0 + 1) * piece)
                value = jnp.concatenate([total(unit, arrivals, q) * slot_weight, tail], axis=0)
                high = value.astype(BF16)
                low = (value - high.astype(F32)).astype(BF16)
                m = jnp.concatenate([main16, pick[p]], axis=0)
                spread = dot(m, high, TN_DIMS) + dot(m, low, TN_DIMS)
                out[:, at] = (gbuf[:, at].astype(F32) + spread).astype(BF16)

    for copy in copies:
        copy.wait_send()


def solution(mesh):
    def on_device(grad_out, parked_inputs, route_ids, route_probs, flight_expert, w_gate, w_up, w_down):
        features = grad_out.shape[1]
        half = features // 2
        hc, piece = half // 2, half // PIECES
        vmem = pltpu.VMEM
        ring_scratch, second_scratch = [], []
        for _ in range(2):
            for width in (3 * piece, piece):
                ring_scratch += [vmem((4, 128, width), BF16), vmem((64, width), BF16), vmem((64, width), BF16),
                                 vmem((128, width), BF16), vmem((128, width), BF16)]
                second_scratch += [vmem((4, 32, width), BF16), vmem((3, 32, width), BF16)]
        scratch = [
            vmem((TOK, half), BF16), vmem((TOK, half), BF16),
            vmem((ROWS, half), BF16), vmem((ROWS, half), BF16),
            vmem((256, piece), BF16), vmem((256, piece), BF16),
            vmem((3, FFD, half), BF16), vmem((3, 3, 2, FFD, half), BF16), vmem((3, FFD, half), BF16),
            vmem((ROWS, half), F32),
            vmem((5, ROWS, 384), F32), vmem((5, ROWS, 384), F32),
            vmem((ROWS, 256), BF16),
            *ring_scratch, *second_scratch,
            vmem((4, 16, hc), BF16), vmem((3, 16, hc), BF16),
            vmem((4, 16, piece), BF16), vmem((3, 16, piece), BF16),
            pltpu.SemaphoreType.DMA((NUM_SEMS,)), pltpu.SemaphoreType.DMA((NUM_SEMS,)),
            pltpu.SemaphoreType.DMA((5,)),
        ]
        any_space = pl.BlockSpec(memory_space=pl.ANY)
        in_vmem = pl.BlockSpec(memory_space=pltpu.VMEM)

        def body(*refs):
            kernel(half, *refs)

        return pl.pallas_call(
            body,
            out_shape=jax.ShapeDtypeStruct((TOK, half), BF16),
            in_specs=[pl.BlockSpec(memory_space=pltpu.SMEM), in_vmem, in_vmem,
                      any_space, any_space, any_space, any_space, any_space],
            out_specs=in_vmem,
            scratch_shapes=scratch,
            compiler_params=pltpu.CompilerParams(
                collective_id=0, has_side_effects=True, vmem_limit_bytes=60 * 1024 * 1024),
            cost_estimate=pl.CostEstimate(
                flops=10 * ROWS * 8 * FFD * half, bytes_accessed=10_000_000, transcendentals=ROWS * 512),
            name="routed_swiglu_backward",
        )(flight_expert, route_ids.T, route_probs.T, grad_out, parked_inputs, w_gate.T, w_up.T, w_down)

    in_specs = (
        P("ep", None),
        P("swap", "ep", None),
        P("ep", None),
        P("ep", None),
        P(),
        P(None, "ep"),
        P(None, "ep"),
        P("ep", None),
    )
    return jax.shard_map(
        on_device, mesh=mesh, in_specs=in_specs, out_specs=P("ep", "swap"), check_vma=False
    )
```

```python
import jax
import jax.numpy as jnp
from jax import lax
from jax.experimental import pallas as pl
from jax.experimental.pallas import tpu as pltpu
from jax.sharding import PartitionSpec as P

MESH = pl.DeviceIdType.MESH
BF16 = jnp.bfloat16
F32 = jnp.float32

CAP = 34
TOK = 128
FFD = 64
NX, NY, NZ = 4, 4, 8
MAIN = 32
ROWS = 16 * CAP
TAIL0 = 16 * MAIN
PIECES = 8
NUM_SEMS = 128
NT_DIMS = (((1,), (1,)), ((), ()))
NN_DIMS = (((1,), (0,)), ((), ()))
TN_DIMS = (((0,), (0,)), ((), ()))


def dot(a, b, dims=NN_DIMS):
    return lax.dot_general(a, b, dims, preferred_element_type=F32)


def iota(shape, dim):
    return lax.broadcasted_iota(jnp.int32, shape, dim)


def kernel(half, fe, ids, probs, grad, parked, wg, wu, wd, out,
           gbuf, pbuf, rx, rdy, tx, tdy, w0, wp, wf, acc, ps, pr, dbuf,
           sa_0, rta_0, rba_0, rla_0, rra_0, sa_1, rta_1, rba_1, rla_1, rra_1,
           sb_0, rtb_0, rbb_0, rlb_0, rrb_0, sb_1, rtb_1, rbb_1, rlb_1, rrb_1,
           sa2_0, ra2_0, sa2_1, ra2_1, sb2_0, rb2_0, sb2_1, rb2_1,
           t1, t1top, t1bottom, t1left, t1right, t2, t2r, acc_dh, send_sem, recv_sem, local_sem):
    piece = half // PIECES
    hc = half // 2
    core = lax.axis_index("swap")
    ep = lax.axis_index("ep")
    y = ep % NY
    z = (ep // NY) % NZ
    x = ep // (NY * NZ)

    def chip(dx, dy, dz):
        place = (((x + dx + NX) % NX) * NZ + (z + dz + NZ) % NZ) * NY + (y + dy + NY) % NY
        return (core, place)

    xp, xm = chip(1, 0, 0), chip(-1, 0, 0)
    yp, ym = chip(0, 1, 0), chip(0, -1, 0)
    zp, zm = chip(0, 0, 1), chip(0, 0, -1)
    xf, yf = chip(2, 0, 0), chip(0, 2, 0)
    a_refs = [(sa_0, rta_0, rba_0, rla_0, rra_0), (sa_1, rta_1, rba_1, rla_1, rra_1)]
    b_refs = [(sb_0, rtb_0, rbb_0, rlb_0, rrb_0), (sb_1, rtb_1, rbb_1, rlb_1, rrb_1)]
    sa2, ra2, sb2, rb2 = (sa2_0, sa2_1), (ra2_0, ra2_1), (sb2_0, sb2_1), (rb2_0, rb2_1)
    other = (1 - core, ep)

    copies, left_already = [], []

    def gone(copy):
        copy.wait_send()
        left_already.append(copy)

    def send(src, dst, device):
        k = len(copies)
        copy = pltpu.make_async_remote_copy(
            src_ref=src, dst_ref=dst, send_sem=send_sem.at[k], recv_sem=recv_sem.at[k],
            device_id=device, device_id_type=MESH)
        copies.append(copy)
        copy.start()
        return copy

    cols = pl.ds(pl.multiple_of(core * half, half), half)
    local = [
        pltpu.make_async_copy(parked.at[0], pbuf, local_sem.at[0]),
        pltpu.make_async_copy(grad.at[:, cols], gbuf, local_sem.at[1]),
        pltpu.make_async_copy(wg.at[:, cols], w0.at[0], local_sem.at[2]),
        pltpu.make_async_copy(wu.at[:, cols], w0.at[1], local_sem.at[3]),
        pltpu.make_async_copy(wd.at[:, cols], w0.at[2], local_sem.at[4]),
    ]
    barrier = pltpu.get_barrier_semaphore()
    for peer in (xp, xm, yp, ym, zp, zm, xf, yf, other):
        pl.semaphore_signal(barrier, inc=1, device_id=peer, device_id_type=MESH)
    for copy in local[2:] + local[:2]:
        copy.start()

    hits = ids[...] == fe[0]
    weight = jnp.sum(jnp.where(hits, probs[...], 0.0), axis=0, keepdims=True)
    flags = jnp.max(hits.astype(F32), axis=0, keepdims=True)
    before = (iota((TOK, TOK), 0) < iota((TOK, TOK), 1)).astype(F32).astype(BF16)
    ranks = dot(jnp.broadcast_to(flags, (16, TOK)).astype(BF16), before)[0:1]

    def match_of(slot, extra=None):
        rank_is = jnp.broadcast_to(ranks, slot.shape) == slot.astype(F32)
        m = jnp.where(rank_is, jnp.broadcast_to(flags, slot.shape), 0.0)
        if extra is not None:
            m = jnp.where(extra, m, 0.0)
        return m

    match_main = match_of(iota((MAIN, TOK), 0))
    tail_row = iota((16, TOK), 0)
    tail_slot = MAIN + tail_row % 2
    match_tail = match_of(tail_slot)
    pick = [match_of(tail_slot, tail_row // 2 == p).astype(BF16) for p in range(PIECES)]
    main16 = match_main.astype(BF16)

    def choose(src, rows, tails):
        rows[0:MAIN, :] = dot(main16, src[...]).astype(BF16)
        t = dot(pick[0], src[:, 0:piece])
        for p in range(1, PIECES):
            t = t + dot(pick[p], src[:, p * piece:(p + 1) * piece])
        tails[0:16, :] = t.astype(BF16)

    for copy in local[2:]:
        copy.wait()
    pl.semaphore_wait(barrier, 9)

    gu, dn = pl.ds(0, 2), pl.ds(2, 1)

    def ring(source, g, part, side):
        return send(source, wp.at[g, part, side], zp if side == 0 else zm)

    arrived = {}
    for part, name in ((gu, "gu"), (dn, "dn")):
        for side in (0, 1):
            arrived[0, name, side] = ring(w0.at[part], 0, part, side)

    def rows_of(s, n=1):
        return pl.ds(MAIN * s, MAIN * n)

    def tails_of(s, n=1):
        return pl.ds(16 * s, 16 * n)

    local[0].wait()
    choose(pbuf, rx, tx)
    px = [send(rx.at[rows_of(0)], rx.at[rows_of(3)], xp),
          send(rx.at[rows_of(0)], rx.at[rows_of(1)], xm),
          send(tx.at[tails_of(0)], tx.at[tails_of(3)], xp),
          send(tx.at[tails_of(0)], tx.at[tails_of(1)], xm)]
    local[1].wait()
    choose(gbuf, rdy, tdy)
    pd = [send(rdy.at[rows_of(0)], rdy.at[rows_of(12)], yp),
          send(rdy.at[rows_of(0)], rdy.at[rows_of(4)], ym),
          send(tdy.at[tails_of(0)], tdy.at[tails_of(12)], yp),
          send(tdy.at[tails_of(0)], tdy.at[tails_of(4)], ym)]

    def forward_rows(first, rows, tails, s3, s1, s2, plus, minus):
        for copy in first:
            copy.wait_recv()
        return [send(rows.at[pl.ds(MAIN * s3, 16)], rows.at[pl.ds(MAIN * s2, 16)], plus),
                send(rows.at[pl.ds(MAIN * s1 + 16, 16)], rows.at[pl.ds(MAIN * s2 + 16, 16)], minus),
                send(tails.at[tails_of(s1)], tails.at[tails_of(s2)], minus)]

    fx = forward_rows(px, rx, tx, 3, 1, 2, xp, xm)
    fd = forward_rows(pd, rdy, tdy, 12, 4, 8, yp, ym)
    for copy in fx:
        copy.wait_recv()
    px = [send(rx.at[rows_of(0, 4)], rx.at[rows_of(12, 4)], yp),
          send(rx.at[rows_of(0, 4)], rx.at[rows_of(4, 4)], ym),
          send(tx.at[tails_of(0, 4)], tx.at[tails_of(12, 4)], yp),
          send(tx.at[tails_of(0, 4)], tx.at[tails_of(4, 4)], ym)]
    for copy in fd:
        copy.wait_recv()
    pd_plus, pd_minus = [], []
    for j in range(4):
        pd_plus.append((send(rdy.at[rows_of(4 * j)], rdy.at[rows_of(4 * j + 3)], xp),
                        send(tdy.at[tails_of(4 * j)], tdy.at[tails_of(4 * j + 3)], xp)))
        pd_minus.append((send(rdy.at[rows_of(4 * j)], rdy.at[rows_of(4 * j + 1)], xm),
                         send(tdy.at[tails_of(4 * j)], tdy.at[tails_of(4 * j + 1)], xm)))

    def forward_weights(g, name, part):
        for side in (0, 1):
            arrived[g - 1, name, side].wait_recv()
            arrived[g, name, side] = ring(wp.at[g - 1, part, side], g, part, side)

    forward_weights(1, "gu", gu)

    for copy in px:
        copy.wait_recv()
    last = [send(rx.at[rows_of(12, 2)], rx.at[rows_of(8, 2)], yp),
            send(rx.at[rows_of(6, 2)], rx.at[rows_of(10, 2)], ym),
            send(tx.at[tails_of(12, 2)], tx.at[tails_of(8, 2)], yp),
            send(tx.at[tails_of(6, 2)], tx.at[tails_of(10, 2)], ym)]
    for pair in pd_plus + pd_minus:
        for copy in pair:
            copy.wait_recv()
    for j in range(4):
        s, to = (4 * j + 3, xp) if j < 2 else (4 * j + 1, xm)
        last.append(send(rdy.at[rows_of(s)], rdy.at[rows_of(4 * j + 2)], to))
        last.append(send(tdy.at[tails_of(s)], tdy.at[tails_of(4 * j + 2)], to))
    forward_weights(1, "dn", dn)
    for copy in last:
        copy.wait_recv()

    row, col = iota((MAIN, 256), 0), iota((MAIN, 256), 1)
    block = row // 2
    base = 16 * (4 * (block % 4) + block // 4) + row % 2
    for p in range(PIECES):
        e = jnp.where(col == base + 2 * p, 1.0, 0.0).astype(BF16)
        for tails, rows in ((tx, rx), (tdy, rdy)):
            rows[TAIL0:ROWS, p * piece:(p + 1) * piece] = dot(e, tails[...]).astype(BF16)

    def weights_of(g):
        if g == 0 or g == 4:
            w = w0 if g == 0 else wf
            return w[0:2].reshape(2 * FFD, half), w[2]
        return wp[g - 1, 0:2].reshape(4 * FFD, half), wp[g - 1, 2].reshape(2 * FFD, half)

    def width_of(g):
        return FFD if g in (0, 4) else 2 * FFD

    def partial_gate(g):
        wgu, _ = weights_of(g)

        @pl.loop(0, 2)
        def _(m):
            rows = pl.ds(pl.multiple_of(m * (ROWS // 2), 16), ROWS // 2)
            ps[g, rows, 0:2 * width_of(g)] = dot(rx[rows, :], wgu, NT_DIMS)

    def partial_dhid(g):
        _, wdn = weights_of(g)
        width = width_of(g)

        @pl.loop(0, 2)
        def _(m):
            rows = pl.ds(pl.multiple_of(m * (ROWS // 2), 16), ROWS // 2)
            dh = dot(rdy[rows, :], wdn, NT_DIMS)
            if width == FFD:
                dh = jnp.concatenate([dh, jnp.zeros_like(dh)], axis=1)
            ps[g, rows, 2 * width:2 * width + 128] = dh

    def exchange(g):
        used = pl.ds(0, 2 * width_of(g) + 128)
        return send(ps.at[g, :, used], pr.at[g, :, used], other)

    def finish(g, begun, lo=0, hi=ROWS // 32):
        for copy in begun:
            copy.wait_recv()
        width = width_of(g)

        @pl.loop(lo, hi)
        def _(m):
            rows = pl.ds(pl.multiple_of(m * 32, 32), 32)
            total = ps[g, rows, 0:2 * width + 128] + pr[g, rows, 0:2 * width + 128]
            gate, up = total[:, 0:width], total[:, width:2 * width]
            dhid = total[:, 2 * width:3 * width]
            s = 1.0 / (1.0 + jnp.exp(-gate))
            d_up = dhid * gate * s
            d_gate = dhid * up * s * (1.0 + gate * (1.0 - s))
            dbuf[rows, 0:2 * width] = jnp.concatenate([d_gate, d_up], axis=1).astype(BF16)

    tile = half // 6

    def back_tiles(g):
        width = width_of(g)

        @pl.loop(0, half // tile)
        def _(n):
            at = pl.ds(pl.multiple_of(n * tile, tile), tile)
            if g == 0:
                w = w0[0:2, :, at].reshape(2 * FFD, tile)
            else:
                w = wp[g - 1, 0:2, :, :, at].reshape(4 * FFD, tile)
            value = dot(dbuf[:, 0:2 * width], w)
            if g == 0:
                acc[:, at] = value
            else:
                acc[:, at] += value

    def begin(g):
        partial_gate(g)
        partial_dhid(g)
        return exchange(g)

    begun0, begun1 = begin(0), begin(1)
    forward_weights(2, "gu", gu)
    finish(0, [begun0])
    back_tiles(0)
    finish(1, [begun1])
    back_tiles(1)
    forward_weights(2, "dn", dn)
    begun2 = begin(2)
    finish(2, [begun2])
    back_tiles(2)

    def forward_far(name, part):
        result = []
        for side in (0, 1):
            arrived[2, name, side].wait_recv()
            hid = pl.ds(32 * side, 32)
            to = zp if side == 0 else zm
            if name == "gu":
                result.append(send(wp.at[2, part, side, hid], wf.at[part, hid], to))
            else:
                result.append([send(wp.at[2, part, side, hid, pl.ds(lo, hc)], wf.at[part, hid, pl.ds(lo, hc)], to)
                               for lo in (0, hc)])
        return result

    far_gu = forward_far("gu", gu)
    partial_gate(3)
    far_dn = forward_far("dn", dn)
    partial_dhid(3)
    finish(3, [exchange(3)])
    back_tiles(3)
    for copy in far_gu:
        copy.wait_recv()
    partial_gate(4)
    far_gate = send(ps.at[4, :, pl.ds(0, 128)], pr.at[4, :, pl.ds(0, 128)], other)
    for pair in far_dn:
        pair[0].wait_recv()
    acc_dh[...] = dot(rdy[:, 0:hc], wf[2, :, 0:hc], NT_DIMS)
    for pair in far_dn:
        pair[1].wait_recv()
    far_dhid = []
    for first, count in ((0, 288), (288, 256)):
        dh = acc_dh[first:first + count, :] + dot(rdy[first:first + count, hc:half], wf[2, :, hc:half], NT_DIMS)
        ps[4, first:first + count, 128:256] = jnp.concatenate([dh, jnp.zeros_like(dh)], axis=1)
        at = (4, pl.ds(first, count), pl.ds(128, 128))
        far_dhid.append(send(ps.at[at], pr.at[at], other))
    finish(4, [far_gate, far_dhid[0]], 0, 9)
    finish(4, [far_dhid[1]], 9, 17)

    def add(a, b):
        return (a.astype(F32) + b.astype(F32)).astype(BF16)

    def start_ring(ring):
        unit, top, bottom, left, right, plus, minus = ring
        up, down = pl.ds(0, 64), pl.ds(64, 64)
        return [send(unit.at[2, up], top, plus), send(unit.at[2, down], bottom, minus)]

    def rest_ring(ring):
        unit, top, bottom, left, right, plus, minus = ring
        up, down = pl.ds(0, 64), pl.ds(64, 64)
        return [send(unit.at[1, down], left.at[down], plus), send(unit.at[3, up], right.at[up], minus)]

    def turn_ring(begun, ends, ring):
        unit, top, bottom, left, right, plus, minus = ring
        up, down = pl.ds(0, 64), pl.ds(64, 64)
        begun[0].wait_recv()
        unit[1, up] = add(unit[1, up], top[...])
        ends.append(send(unit.at[1, up], left.at[up], plus))
        begun[1].wait_recv()
        unit[3, down] = add(unit[3, down], bottom[...])
        ends.append(send(unit.at[3, down], right.at[down], minus))

    def second(ends, ring, unit, arrivals, plus, minus, far):
        own, _, _, left, right, _, _ = ring
        for copy in ends:
            copy.wait_recv()
        for k in (2, 1, 3, 0):
            rows = slice(32 * k, 32 * k + 32)
            unit[k] = (own[0, rows].astype(F32) + left[rows].astype(F32) + right[rows].astype(F32)).astype(BF16)
        return scatter(unit, arrivals, plus, minus, far)

    def scatter(unit, arrivals, plus, minus, far):
        return [send(unit.at[2], arrivals.at[1], far),
                send(unit.at[1], arrivals.at[0], plus), send(unit.at[3], arrivals.at[2], minus)]

    rings_a = [a + (xp, xm) for a in a_refs]
    rings_b = [b + (yp, ym) for b in b_refs]

    def last_tiles(c, is_a):
        n0, n1 = (0, 3) if c == 0 else (3, 4)
        for n in range(n0, n1):
            p = n if is_a else n + 4
            at = slice(p * piece, (p + 1) * piece)
            to = slice((n - n0) * piece, (n - n0 + 1) * piece)
            value = acc[0:TAIL0, at] + dot(dbuf[0:TAIL0, 0:2 * FFD], wf[0:2, :, at].reshape(2 * FFD, piece))
            for i in range(4):
                for j in range(4):
                    s = 4 * j + i
                    block = value[MAIN * s:MAIN * s + MAIN].astype(BF16)
                    if is_a:
                        rings_a[c][0][i, 32 * j:32 * j + 32, to] = block
                    else:
                        rings_b[c][0][j, 32 * i:32 * i + 32, to] = block

    begun_a, begun_b, ends_a, ends_b = [], [], [], []
    last_tiles(0, False)
    begun_b.append(start_ring(rings_b[0]))
    last_tiles(0, True)
    begun_a.append(start_ring(rings_a[0]))

    low_half, high_half = pl.ds(0, hc // 2), pl.ds(hc // 2, hc // 2)
    tails = acc[TAIL0:ROWS, :] + dot(dbuf[TAIL0:ROWS, 0:2 * FFD], wf[0:2].reshape(2 * FFD, half))
    for i in range(4):
        t = tails[8 * i:8 * i + 8, :]
        t1[i] = jnp.concatenate([t[:, 0:hc], t[:, hc:half]], axis=0).astype(BF16)
    tail_top = send(t1.at[2, :, low_half], t1top, xp)
    tail_bottom = send(t1.at[2, :, high_half], t1bottom, xm)

    last_tiles(1, False)
    begun_b.append(start_ring(rings_b[1]))
    last_tiles(1, True)
    begun_a.append(start_ring(rings_a[1]))

    tail_ends = [send(t1.at[1, :, high_half], t1left.at[:, high_half], xp),
                 send(t1.at[3, :, low_half], t1right.at[:, low_half], xm)]
    for copy in begun_b[0] + begun_a[0]:
        gone(copy)
    ends_b.append(rest_ring(rings_b[0]))
    ends_a.append(rest_ring(rings_a[0]))
    tail_top.wait_recv()
    t1[1, :, low_half] = add(t1[1, :, low_half], t1top[...])
    tail_ends.append(send(t1.at[1, :, low_half], t1left.at[:, low_half], xp))
    tail_bottom.wait_recv()
    t1[3, :, high_half] = add(t1[3, :, high_half], t1bottom[...])
    tail_ends.append(send(t1.at[3, :, high_half], t1right.at[:, high_half], xm))
    turn_ring(begun_b[0], ends_b[0], rings_b[0])
    turn_ring(begun_a[0], ends_a[0], rings_a[0])
    ends_b.append(rest_ring(rings_b[1]))
    ends_a.append(rest_ring(rings_a[1]))
    turn_ring(begun_b[1], ends_b[1], rings_b[1])
    turn_ring(begun_a[1], ends_a[1], rings_a[1])

    for copy in tail_ends:
        copy.wait_recv()
    tail = (t1[0].astype(F32) + t1left[...].astype(F32) + t1right[...].astype(F32)).astype(BF16)
    row, col = iota((64, 16), 0), iota((64, 16), 1)
    p_of = (row % 16) // 2
    wanted = 8 * (p_of // 4) + 2 * (row // 16) + row % 2
    packed = jnp.zeros((64, piece), F32)
    for q in range(4):
        f = jnp.where((col == wanted) & (p_of % 4 == q), 1.0, 0.0).astype(BF16)
        packed = packed + dot(f, tail[:, q * piece:(q + 1) * piece])
    t2[...] = packed.astype(BF16).reshape(4, 16, piece)
    tail_ends = scatter(t2, t2r, yp, ym, yf)

    last_b, last_a = [], []
    for c in range(2):
        last_b.append(second(ends_b[c], rings_b[c], sb2[c], rb2[c], xp, xm, xf))
        last_a.append(second(ends_a[c], rings_a[c], sa2[c], ra2[c], yp, ym, yf))

    slot_weight = 0.5 * jnp.sum(match_main * weight, axis=1, keepdims=True)
    tail_weight = 0.5 * jnp.sum(match_tail * weight, axis=1, keepdims=True)

    def total(unit, arrivals, at=None):
        if at is None:
            return unit[0].astype(F32) + arrivals[0].astype(F32) + arrivals[1].astype(F32) + arrivals[2].astype(F32)
        return (unit[0, :, at].astype(F32) + arrivals[0, :, at].astype(F32)
                + arrivals[1, :, at].astype(F32) + arrivals[2, :, at].astype(F32))

    for copy in tail_ends:
        copy.wait_recv()
    tail = total(t2, t2r) * tail_weight
    for c in range(2):
        for ends, unit, arrivals, p0 in ((last_b[c], sb2[c], rb2[c], 4), (last_a[c], sa2[c], ra2[c], 0)):
            for copy in ends:
                copy.wait_recv()
            n0, n1 = (0, 3) if c == 0 else (3, 4)
            for n in range(n0, n1):
                p = p0 + n
                at = slice(p * piece, (p + 1) * piece)
                q = slice((n - n0) * piece, (n - n0 + 1) * piece)
                value = jnp.concatenate([total(unit, arrivals, q) * slot_weight, tail], axis=0)
                high = value.astype(BF16)
                low = (value - high.astype(F32)).astype(BF16)
                m = jnp.concatenate([main16, pick[p]], axis=0)
                spread = dot(m, high, TN_DIMS) + dot(m, low, TN_DIMS)
                out[:, at] = (gbuf[:, at].astype(F32) + spread).astype(BF16)

    for copy in copies:
        if not any(copy is other_copy for other_copy in left_already):
            copy.wait_send()


def solution(mesh):
    def on_device(grad_out, parked_inputs, route_ids, route_probs, flight_expert, w_gate, w_up, w_down):
        features = grad_out.shape[1]
        half = features // 2
        hc, piece = half // 2, half // PIECES
        vmem = pltpu.VMEM
        ring_scratch, second_scratch = [], []
        for _ in range(2):
            for width in (3 * piece, piece):
                ring_scratch += [vmem((4, 128, width), BF16), vmem((64, width), BF16), vmem((64, width), BF16),
                                 vmem((128, width), BF16), vmem((128, width), BF16)]
                second_scratch += [vmem((4, 32, width), BF16), vmem((3, 32, width), BF16)]
        scratch = [
            vmem((TOK, half), BF16), vmem((TOK, half), BF16),
            vmem((ROWS, half), BF16), vmem((ROWS, half), BF16),
            vmem((256, piece), BF16), vmem((256, piece), BF16),
            vmem((3, FFD, half), BF16), vmem((3, 3, 2, FFD, half), BF16), vmem((3, FFD, half), BF16),
            vmem((ROWS, half), F32),
            vmem((5, ROWS, 384), F32), vmem((5, ROWS, 384), F32),
            vmem((ROWS, 256), BF16),
            *ring_scratch, *second_scratch,
            vmem((4, 16, hc), BF16), vmem((16, hc // 2), BF16), vmem((16, hc // 2), BF16),
            vmem((16, hc), BF16), vmem((16, hc), BF16),
            vmem((4, 16, piece), BF16), vmem((3, 16, piece), BF16),
            vmem((ROWS, FFD), F32),
            pltpu.SemaphoreType.DMA((NUM_SEMS,)), pltpu.SemaphoreType.DMA((NUM_SEMS,)),
            pltpu.SemaphoreType.DMA((5,)),
        ]
        any_space = pl.BlockSpec(memory_space=pl.ANY)
        in_vmem = pl.BlockSpec(memory_space=pltpu.VMEM)

        def body(*refs):
            kernel(half, *refs)

        return pl.pallas_call(
            body,
            out_shape=jax.ShapeDtypeStruct((TOK, half), BF16),
            in_specs=[pl.BlockSpec(memory_space=pltpu.SMEM), in_vmem, in_vmem,
                      any_space, any_space, any_space, any_space, any_space],
            out_specs=in_vmem,
            scratch_shapes=scratch,
            compiler_params=pltpu.CompilerParams(
                collective_id=0, has_side_effects=True, vmem_limit_bytes=60 * 1024 * 1024),
            cost_estimate=pl.CostEstimate(
                flops=10 * ROWS * 8 * FFD * half, bytes_accessed=10_000_000, transcendentals=ROWS * 512),
            name="routed_swiglu_backward",
        )(flight_expert, route_ids.T, route_probs.T, grad_out, parked_inputs, w_gate.T, w_up.T, w_down)

    in_specs = (
        P("ep", None),
        P("swap", "ep", None),
        P("ep", None),
        P("ep", None),
        P(),
        P(None, "ep"),
        P(None, "ep"),
        P("ep", None),
    )
    return jax.shard_map(
        on_device, mesh=mesh, in_specs=in_specs, out_specs=P("ep", "swap"), check_vma=False
    )
```

```python
import jax
import jax.numpy as jnp
from jax import lax
from jax.experimental import pallas as pl
from jax.experimental.pallas import tpu as pltpu
from jax.sharding import PartitionSpec as P

MESH = pl.DeviceIdType.MESH
BF16 = jnp.bfloat16
F32 = jnp.float32

CAP = 34
TOK = 128
FFD = 64
NX, NY, NZ = 4, 4, 8
MAIN = 32
ROWS = 16 * CAP
TAIL0 = 16 * MAIN
PIECES = 8
NUM_SEMS = 128
NT_DIMS = (((1,), (1,)), ((), ()))
NN_DIMS = (((1,), (0,)), ((), ()))
TN_DIMS = (((0,), (0,)), ((), ()))


def dot(a, b, dims=NN_DIMS):
    return lax.dot_general(a, b, dims, preferred_element_type=F32)


def iota(shape, dim):
    return lax.broadcasted_iota(jnp.int32, shape, dim)


def kernel(half, fe, ids, probs, grad, parked, wg, wu, wd, out,
           gbuf, pbuf, rx, rdy, tx, tdy, w0, wp, wf, acc, ps, pr, dbuf,
           sa_0, rta_0, rba_0, rla_0, rra_0, sa_1, rta_1, rba_1, rla_1, rra_1,
           sb_0, rtb_0, rbb_0, rlb_0, rrb_0, sb_1, rtb_1, rbb_1, rlb_1, rrb_1,
           sa2_0, ra2_0, sa2_1, ra2_1, sb2_0, rb2_0, sb2_1, rb2_1,
           t1, t1top, t1bottom, t1left, t1right, t2, t2r, acc_dh, send_sem, recv_sem, local_sem):
    piece = half // PIECES
    hc = half // 2
    core = lax.axis_index("swap")
    ep = lax.axis_index("ep")
    y = ep % NY
    z = (ep // NY) % NZ
    x = ep // (NY * NZ)

    def chip(dx, dy, dz):
        place = (((x + dx + NX) % NX) * NZ + (z + dz + NZ) % NZ) * NY + (y + dy + NY) % NY
        return (core, place)

    xp, xm = chip(1, 0, 0), chip(-1, 0, 0)
    yp, ym = chip(0, 1, 0), chip(0, -1, 0)
    zp, zm = chip(0, 0, 1), chip(0, 0, -1)
    xf, yf = chip(2, 0, 0), chip(0, 2, 0)
    a_refs = [(sa_0, rta_0, rba_0, rla_0, rra_0), (sa_1, rta_1, rba_1, rla_1, rra_1)]
    b_refs = [(sb_0, rtb_0, rbb_0, rlb_0, rrb_0), (sb_1, rtb_1, rbb_1, rlb_1, rrb_1)]
    sa2, ra2, sb2, rb2 = (sa2_0, sa2_1), (ra2_0, ra2_1), (sb2_0, sb2_1), (rb2_0, rb2_1)
    other = (1 - core, ep)

    copies, left_already = [], []

    def gone(copy):
        copy.wait_send()
        left_already.append(copy)

    def send(src, dst, device):
        k = len(copies)
        copy = pltpu.make_async_remote_copy(
            src_ref=src, dst_ref=dst, send_sem=send_sem.at[k], recv_sem=recv_sem.at[k],
            device_id=device, device_id_type=MESH)
        copies.append(copy)
        copy.start()
        return copy

    cols = pl.ds(pl.multiple_of(core * half, half), half)
    local = [
        pltpu.make_async_copy(parked.at[0], pbuf, local_sem.at[0]),
        pltpu.make_async_copy(grad.at[:, cols], gbuf, local_sem.at[1]),
        pltpu.make_async_copy(wg.at[:, cols], w0.at[0], local_sem.at[2]),
        pltpu.make_async_copy(wu.at[:, cols], w0.at[1], local_sem.at[3]),
        pltpu.make_async_copy(wd.at[:, cols], w0.at[2], local_sem.at[4]),
    ]
    barrier = pltpu.get_barrier_semaphore()
    for peer in (xp, xm, yp, ym, zp, zm, xf, yf, other):
        pl.semaphore_signal(barrier, inc=1, device_id=peer, device_id_type=MESH)
    for copy in local[2:] + local[:2]:
        copy.start()

    hits = ids[...] == fe[0]
    weight = jnp.sum(jnp.where(hits, probs[...], 0.0), axis=0, keepdims=True)
    flags = jnp.max(hits.astype(F32), axis=0, keepdims=True)
    before = (iota((TOK, TOK), 0) < iota((TOK, TOK), 1)).astype(F32).astype(BF16)
    ranks = dot(jnp.broadcast_to(flags, (16, TOK)).astype(BF16), before)[0:1]

    def match_of(slot, extra=None):
        rank_is = jnp.broadcast_to(ranks, slot.shape) == slot.astype(F32)
        m = jnp.where(rank_is, jnp.broadcast_to(flags, slot.shape), 0.0)
        if extra is not None:
            m = jnp.where(extra, m, 0.0)
        return m

    match_main = match_of(iota((MAIN, TOK), 0))
    tail_row = iota((16, TOK), 0)
    tail_slot = MAIN + tail_row % 2
    match_tail = match_of(tail_slot)
    pick = [match_of(tail_slot, tail_row // 2 == p).astype(BF16) for p in range(PIECES)]
    main16 = match_main.astype(BF16)

    def choose(src, rows, tails):
        rows[0:MAIN, :] = dot(main16, src[...]).astype(BF16)
        t = dot(pick[0], src[:, 0:piece])
        for p in range(1, PIECES):
            t = t + dot(pick[p], src[:, p * piece:(p + 1) * piece])
        tails[0:16, :] = t.astype(BF16)

    for copy in local[2:]:
        copy.wait()
    pl.semaphore_wait(barrier, 9)

    gu, dn = pl.ds(0, 2), pl.ds(2, 1)

    def ring(source, g, part, side):
        return send(source, wp.at[g, part, side], zp if side == 0 else zm)

    arrived = {}
    for part, name in ((gu, "gu"), (dn, "dn")):
        for side in (0, 1):
            arrived[0, name, side] = ring(w0.at[part], 0, part, side)

    def rows_of(s, n=1):
        return pl.ds(MAIN * s, MAIN * n)

    def tails_of(s, n=1):
        return pl.ds(16 * s, 16 * n)

    local[0].wait()
    choose(pbuf, rx, tx)
    px = [send(rx.at[rows_of(0)], rx.at[rows_of(3)], xp),
          send(rx.at[rows_of(0)], rx.at[rows_of(1)], xm),
          send(tx.at[tails_of(0)], tx.at[tails_of(3)], xp),
          send(tx.at[tails_of(0)], tx.at[tails_of(1)], xm)]
    local[1].wait()
    choose(gbuf, rdy, tdy)
    pd = [send(rdy.at[rows_of(0)], rdy.at[rows_of(12)], yp),
          send(rdy.at[rows_of(0)], rdy.at[rows_of(4)], ym),
          send(tdy.at[tails_of(0)], tdy.at[tails_of(12)], yp),
          send(tdy.at[tails_of(0)], tdy.at[tails_of(4)], ym)]

    def forward_rows(first, rows, tails, s3, s1, s2, plus, minus):
        for copy in first:
            copy.wait_recv()
        return [send(rows.at[pl.ds(MAIN * s3, 16)], rows.at[pl.ds(MAIN * s2, 16)], plus),
                send(rows.at[pl.ds(MAIN * s1 + 16, 16)], rows.at[pl.ds(MAIN * s2 + 16, 16)], minus),
                send(tails.at[tails_of(s1)], tails.at[tails_of(s2)], minus)]

    fx = forward_rows(px, rx, tx, 3, 1, 2, xp, xm)
    fd = forward_rows(pd, rdy, tdy, 12, 4, 8, yp, ym)
    for copy in fx:
        copy.wait_recv()
    px = [send(rx.at[rows_of(0, 4)], rx.at[rows_of(12, 4)], yp),
          send(rx.at[rows_of(0, 4)], rx.at[rows_of(4, 4)], ym),
          send(tx.at[tails_of(0, 4)], tx.at[tails_of(12, 4)], yp),
          send(tx.at[tails_of(0, 4)], tx.at[tails_of(4, 4)], ym)]
    for copy in fd:
        copy.wait_recv()
    pd_plus, pd_minus = [], []
    for j in range(4):
        pd_plus.append((send(rdy.at[rows_of(4 * j)], rdy.at[rows_of(4 * j + 3)], xp),
                        send(tdy.at[tails_of(4 * j)], tdy.at[tails_of(4 * j + 3)], xp)))
        pd_minus.append((send(rdy.at[rows_of(4 * j)], rdy.at[rows_of(4 * j + 1)], xm),
                         send(tdy.at[tails_of(4 * j)], tdy.at[tails_of(4 * j + 1)], xm)))

    def forward_weights(g, name, part):
        for side in (0, 1):
            arrived[g - 1, name, side].wait_recv()
            arrived[g, name, side] = ring(wp.at[g - 1, part, side], g, part, side)

    forward_weights(1, "gu", gu)
    forward_weights(1, "dn", dn)

    for copy in px:
        copy.wait_recv()
    last = [send(rx.at[rows_of(12, 2)], rx.at[rows_of(8, 2)], yp),
            send(rx.at[rows_of(6, 2)], rx.at[rows_of(10, 2)], ym),
            send(tx.at[tails_of(12, 2)], tx.at[tails_of(8, 2)], yp),
            send(tx.at[tails_of(6, 2)], tx.at[tails_of(10, 2)], ym)]
    for pair in pd_plus + pd_minus:
        for copy in pair:
            copy.wait_recv()
    for j in range(4):
        s, to = (4 * j + 3, xp) if j < 2 else (4 * j + 1, xm)
        last.append(send(rdy.at[rows_of(s)], rdy.at[rows_of(4 * j + 2)], to))
        last.append(send(tdy.at[tails_of(s)], tdy.at[tails_of(4 * j + 2)], to))
    for copy in last:
        copy.wait_recv()

    row, col = iota((MAIN, 256), 0), iota((MAIN, 256), 1)
    block = row // 2
    base = 16 * (4 * (block % 4) + block // 4) + row % 2
    for p in range(PIECES):
        e = jnp.where(col == base + 2 * p, 1.0, 0.0).astype(BF16)
        for tails, rows in ((tx, rx), (tdy, rdy)):
            rows[TAIL0:ROWS, p * piece:(p + 1) * piece] = dot(e, tails[...]).astype(BF16)

    def weights_of(g):
        if g == 0 or g == 4:
            w = w0 if g == 0 else wf
            return w[0:2].reshape(2 * FFD, half), w[2]
        return wp[g - 1, 0:2].reshape(4 * FFD, half), wp[g - 1, 2].reshape(2 * FFD, half)

    def width_of(g):
        return FFD if g in (0, 4) else 2 * FFD

    def partial_gate(g):
        wgu, _ = weights_of(g)

        @pl.loop(0, 2)
        def _(m):
            rows = pl.ds(pl.multiple_of(m * (ROWS // 2), 16), ROWS // 2)
            ps[g, rows, 0:2 * width_of(g)] = dot(rx[rows, :], wgu, NT_DIMS)

    def partial_dhid(g):
        _, wdn = weights_of(g)
        width = width_of(g)

        @pl.loop(0, 2)
        def _(m):
            rows = pl.ds(pl.multiple_of(m * (ROWS // 2), 16), ROWS // 2)
            dh = dot(rdy[rows, :], wdn, NT_DIMS)
            if width == FFD:
                dh = jnp.concatenate([dh, jnp.zeros_like(dh)], axis=1)
            ps[g, rows, 2 * width:2 * width + 128] = dh

    def exchange(g):
        used = pl.ds(0, 2 * width_of(g) + 128)
        return send(ps.at[g, :, used], pr.at[g, :, used], other)

    def finish(g, begun, lo=0, hi=ROWS // 32):
        for copy in begun:
            copy.wait_recv()
        width = width_of(g)

        @pl.loop(lo, hi)
        def _(m):
            rows = pl.ds(pl.multiple_of(m * 32, 32), 32)
            total = ps[g, rows, 0:2 * width + 128] + pr[g, rows, 0:2 * width + 128]
            gate, up = total[:, 0:width], total[:, width:2 * width]
            dhid = total[:, 2 * width:3 * width]
            s = 1.0 / (1.0 + jnp.exp(-gate))
            d_up = dhid * gate * s
            d_gate = dhid * up * s * (1.0 + gate * (1.0 - s))
            dbuf[rows, 0:2 * width] = jnp.concatenate([d_gate, d_up], axis=1).astype(BF16)

    tile = half // 6

    def back_tiles(g):
        width = width_of(g)

        @pl.loop(0, half // tile)
        def _(n):
            at = pl.ds(pl.multiple_of(n * tile, tile), tile)
            if g == 0:
                w = w0[0:2, :, at].reshape(2 * FFD, tile)
            else:
                w = wp[g - 1, 0:2, :, :, at].reshape(4 * FFD, tile)
            value = dot(dbuf[:, 0:2 * width], w)
            if g == 0:
                acc[:, at] = value
            else:
                acc[:, at] += value

    def begin(g):
        partial_gate(g)
        partial_dhid(g)
        return exchange(g)

    begun0 = begin(0)
    forward_weights(2, "gu", gu)
    begun1 = begin(1)
    finish(0, [begun0])
    back_tiles(0)
    forward_weights(2, "dn", dn)
    finish(1, [begun1])
    back_tiles(1)
    begun2 = begin(2)
    finish(2, [begun2])
    back_tiles(2)

    def forward_far(name, part):
        result = []
        for side in (0, 1):
            arrived[2, name, side].wait_recv()
            hid = pl.ds(32 * side, 32)
            to = zp if side == 0 else zm
            if name == "gu":
                result.append(send(wp.at[2, part, side, hid], wf.at[part, hid], to))
            else:
                result.append([send(wp.at[2, part, side, hid, pl.ds(lo, hc)], wf.at[part, hid, pl.ds(lo, hc)], to)
                               for lo in (0, hc)])
        return result

    far_gu = forward_far("gu", gu)
    partial_gate(3)
    far_dn = forward_far("dn", dn)
    partial_dhid(3)
    finish(3, [exchange(3)])
    back_tiles(3)
    for copy in far_gu:
        copy.wait_recv()
    partial_gate(4)
    far_gate = send(ps.at[4, :, pl.ds(0, 128)], pr.at[4, :, pl.ds(0, 128)], other)
    for pair in far_dn:
        pair[0].wait_recv()
    acc_dh[...] = dot(rdy[:, 0:hc], wf[2, :, 0:hc], NT_DIMS)
    for pair in far_dn:
        pair[1].wait_recv()
    far_dhid = []
    for first, count in ((0, 288), (288, 256)):
        dh = acc_dh[first:first + count, :] + dot(rdy[first:first + count, hc:half], wf[2, :, hc:half], NT_DIMS)
        ps[4, first:first + count, 128:256] = jnp.concatenate([dh, jnp.zeros_like(dh)], axis=1)
        at = (4, pl.ds(first, count), pl.ds(128, 128))
        far_dhid.append(send(ps.at[at], pr.at[at], other))
    finish(4, [far_gate, far_dhid[0]], 0, 9)
    finish(4, [far_dhid[1]], 9, 17)

    def add(a, b):
        return (a.astype(F32) + b.astype(F32)).astype(BF16)

    def start_ring(ring):
        unit, top, bottom, left, right, plus, minus = ring
        up, down = pl.ds(0, 64), pl.ds(64, 64)
        return [send(unit.at[2, up], top, plus), send(unit.at[2, down], bottom, minus)]

    def rest_ring(ring):
        unit, top, bottom, left, right, plus, minus = ring
        up, down = pl.ds(0, 64), pl.ds(64, 64)
        return [send(unit.at[1, down], left.at[down], plus), send(unit.at[3, up], right.at[up], minus)]

    def turn_ring(begun, ends, ring):
        unit, top, bottom, left, right, plus, minus = ring
        up, down = pl.ds(0, 64), pl.ds(64, 64)
        begun[0].wait_recv()
        unit[1, up] = add(unit[1, up], top[...])
        ends.append(send(unit.at[1, up], left.at[up], plus))
        begun[1].wait_recv()
        unit[3, down] = add(unit[3, down], bottom[...])
        ends.append(send(unit.at[3, down], right.at[down], minus))

    def second(ends, ring, unit, arrivals, plus, minus, far):
        own, _, _, left, right, _, _ = ring
        for copy in ends:
            copy.wait_recv()
        for k in (2, 1, 3, 0):
            rows = slice(32 * k, 32 * k + 32)
            unit[k] = (own[0, rows].astype(F32) + left[rows].astype(F32) + right[rows].astype(F32)).astype(BF16)
        return scatter(unit, arrivals, plus, minus, far)

    def scatter(unit, arrivals, plus, minus, far):
        return [send(unit.at[2], arrivals.at[1], far),
                send(unit.at[1], arrivals.at[0], plus), send(unit.at[3], arrivals.at[2], minus)]

    rings_a = [a + (xp, xm) for a in a_refs]
    rings_b = [b + (yp, ym) for b in b_refs]

    def last_tiles(c, is_a):
        n0, n1 = (0, 2) if c == 0 else (2, 4)
        for n in range(n0, n1):
            p = n if is_a else n + 4
            at = slice(p * piece, (p + 1) * piece)
            to = slice((n - n0) * piece, (n - n0 + 1) * piece)
            value = acc[0:TAIL0, at] + dot(dbuf[0:TAIL0, 0:2 * FFD], wf[0:2, :, at].reshape(2 * FFD, piece))
            for i in range(4):
                for j in range(4):
                    s = 4 * j + i
                    block = value[MAIN * s:MAIN * s + MAIN].astype(BF16)
                    if is_a:
                        rings_a[c][0][i, 32 * j:32 * j + 32, to] = block
                    else:
                        rings_b[c][0][j, 32 * i:32 * i + 32, to] = block

    begun_a, begun_b, ends_a, ends_b = [], [], [], []
    last_tiles(0, False)
    begun_b.append(start_ring(rings_b[0]))
    last_tiles(0, True)
    begun_a.append(start_ring(rings_a[0]))

    low_half, high_half = pl.ds(0, hc // 2), pl.ds(hc // 2, hc // 2)
    tails = acc[TAIL0:ROWS, :] + dot(dbuf[TAIL0:ROWS, 0:2 * FFD], wf[0:2].reshape(2 * FFD, half))
    for i in range(4):
        t = tails[8 * i:8 * i + 8, :]
        t1[i] = jnp.concatenate([t[:, 0:hc], t[:, hc:half]], axis=0).astype(BF16)
    tail_top = send(t1.at[2, :, low_half], t1top, xp)
    tail_bottom = send(t1.at[2, :, high_half], t1bottom, xm)

    last_tiles(1, False)
    begun_b.append(start_ring(rings_b[1]))
    last_tiles(1, True)
    begun_a.append(start_ring(rings_a[1]))

    tail_ends = [send(t1.at[1, :, high_half], t1left.at[:, high_half], xp),
                 send(t1.at[3, :, low_half], t1right.at[:, low_half], xm)]
    for copy in begun_b[0] + begun_a[0]:
        gone(copy)
    ends_b.append(rest_ring(rings_b[0]))
    ends_a.append(rest_ring(rings_a[0]))
    tail_top.wait_recv()
    t1[1, :, low_half] = add(t1[1, :, low_half], t1top[...])
    tail_ends.append(send(t1.at[1, :, low_half], t1left.at[:, low_half], xp))
    tail_bottom.wait_recv()
    t1[3, :, high_half] = add(t1[3, :, high_half], t1bottom[...])
    tail_ends.append(send(t1.at[3, :, high_half], t1right.at[:, high_half], xm))
    turn_ring(begun_b[0], ends_b[0], rings_b[0])
    turn_ring(begun_a[0], ends_a[0], rings_a[0])
    ends_b.append(rest_ring(rings_b[1]))
    ends_a.append(rest_ring(rings_a[1]))
    turn_ring(begun_b[1], ends_b[1], rings_b[1])
    turn_ring(begun_a[1], ends_a[1], rings_a[1])

    for copy in tail_ends:
        copy.wait_recv()
    tail = (t1[0].astype(F32) + t1left[...].astype(F32) + t1right[...].astype(F32)).astype(BF16)
    row, col = iota((64, 16), 0), iota((64, 16), 1)
    p_of = (row % 16) // 2
    wanted = 8 * (p_of // 4) + 2 * (row // 16) + row % 2
    packed = jnp.zeros((64, piece), F32)
    for q in range(4):
        f = jnp.where((col == wanted) & (p_of % 4 == q), 1.0, 0.0).astype(BF16)
        packed = packed + dot(f, tail[:, q * piece:(q + 1) * piece])
    t2[...] = packed.astype(BF16).reshape(4, 16, piece)
    tail_ends = scatter(t2, t2r, yp, ym, yf)

    last_b, last_a = [], []
    for c in range(2):
        last_b.append(second(ends_b[c], rings_b[c], sb2[c], rb2[c], xp, xm, xf))
        last_a.append(second(ends_a[c], rings_a[c], sa2[c], ra2[c], yp, ym, yf))

    slot_weight = 0.5 * jnp.sum(match_main * weight, axis=1, keepdims=True)
    tail_weight = 0.5 * jnp.sum(match_tail * weight, axis=1, keepdims=True)

    def total(unit, arrivals, at=None):
        if at is None:
            return unit[0].astype(F32) + arrivals[0].astype(F32) + arrivals[1].astype(F32) + arrivals[2].astype(F32)
        return (unit[0, :, at].astype(F32) + arrivals[0, :, at].astype(F32)
                + arrivals[1, :, at].astype(F32) + arrivals[2, :, at].astype(F32))

    for copy in tail_ends:
        copy.wait_recv()
    tail = total(t2, t2r) * tail_weight
    for c in range(2):
        for ends, unit, arrivals, p0 in ((last_b[c], sb2[c], rb2[c], 4), (last_a[c], sa2[c], ra2[c], 0)):
            for copy in ends:
                copy.wait_recv()
            n0, n1 = (0, 2) if c == 0 else (2, 4)
            for n in range(n0, n1):
                p = p0 + n
                at = slice(p * piece, (p + 1) * piece)
                q = slice((n - n0) * piece, (n - n0 + 1) * piece)
                value = jnp.concatenate([total(unit, arrivals, q) * slot_weight, tail], axis=0)
                high = value.astype(BF16)
                low = (value - high.astype(F32)).astype(BF16)
                m = jnp.concatenate([main16, pick[p]], axis=0)
                spread = dot(m, high, TN_DIMS) + dot(m, low, TN_DIMS)
                out[:, at] = (gbuf[:, at].astype(F32) + spread).astype(BF16)

    for copy in copies:
        if not any(copy is other_copy for other_copy in left_already):
            copy.wait_send()


def solution(mesh):
    def on_device(grad_out, parked_inputs, route_ids, route_probs, flight_expert, w_gate, w_up, w_down):
        features = grad_out.shape[1]
        half = features // 2
        hc, piece = half // 2, half // PIECES
        vmem = pltpu.VMEM
        ring_scratch, second_scratch = [], []
        for _ in range(2):
            for width in (2 * piece, 2 * piece):
                ring_scratch += [vmem((4, 128, width), BF16), vmem((64, width), BF16), vmem((64, width), BF16),
                                 vmem((128, width), BF16), vmem((128, width), BF16)]
                second_scratch += [vmem((4, 32, width), BF16), vmem((3, 32, width), BF16)]
        scratch = [
            vmem((TOK, half), BF16), vmem((TOK, half), BF16),
            vmem((ROWS, half), BF16), vmem((ROWS, half), BF16),
            vmem((256, piece), BF16), vmem((256, piece), BF16),
            vmem((3, FFD, half), BF16), vmem((3, 3, 2, FFD, half), BF16), vmem((3, FFD, half), BF16),
            vmem((ROWS, half), F32),
            vmem((5, ROWS, 384), F32), vmem((5, ROWS, 384), F32),
            vmem((ROWS, 256), BF16),
            *ring_scratch, *second_scratch,
            vmem((4, 16, hc), BF16), vmem((16, hc // 2), BF16), vmem((16, hc // 2), BF16),
            vmem((16, hc), BF16), vmem((16, hc), BF16),
            vmem((4, 16, piece), BF16), vmem((3, 16, piece), BF16),
            vmem((ROWS, FFD), F32),
            pltpu.SemaphoreType.DMA((NUM_SEMS,)), pltpu.SemaphoreType.DMA((NUM_SEMS,)),
            pltpu.SemaphoreType.DMA((5,)),
        ]
        any_space = pl.BlockSpec(memory_space=pl.ANY)
        in_vmem = pl.BlockSpec(memory_space=pltpu.VMEM)

        def body(*refs):
            kernel(half, *refs)

        return pl.pallas_call(
            body,
            out_shape=jax.ShapeDtypeStruct((TOK, half), BF16),
            in_specs=[pl.BlockSpec(memory_space=pltpu.SMEM), in_vmem, in_vmem,
                      any_space, any_space, any_space, any_space, any_space],
            out_specs=in_vmem,
            scratch_shapes=scratch,
            compiler_params=pltpu.CompilerParams(
                collective_id=0, has_side_effects=True, vmem_limit_bytes=60 * 1024 * 1024),
            cost_estimate=pl.CostEstimate(
                flops=10 * ROWS * 8 * FFD * half, bytes_accessed=10_000_000, transcendentals=ROWS * 512),
            name="routed_swiglu_backward",
        )(flight_expert, route_ids.T, route_probs.T, grad_out, parked_inputs, w_gate.T, w_up.T, w_down)

    in_specs = (
        P("ep", None),
        P("swap", "ep", None),
        P("ep", None),
        P("ep", None),
        P(),
        P(None, "ep"),
        P(None, "ep"),
        P("ep", None),
    )
    return jax.shard_map(
        on_device, mesh=mesh, in_specs=in_specs, out_specs=P("ep", "swap"), check_vma=False
    )
```

```python
import jax
import jax.numpy as jnp
from jax import lax
from jax.experimental import pallas as pl
from jax.experimental.pallas import tpu as pltpu
from jax.sharding import PartitionSpec as P

MESH = pl.DeviceIdType.MESH
BF16 = jnp.bfloat16
F32 = jnp.float32

CAP = 34
TOK = 128
FFD = 64
NX, NY, NZ = 4, 4, 8
MAIN = 32
ROWS = 16 * CAP
TAIL0 = 16 * MAIN
PIECES = 8
NUM_SEMS = 128
NT_DIMS = (((1,), (1,)), ((), ()))
NN_DIMS = (((1,), (0,)), ((), ()))
TN_DIMS = (((0,), (0,)), ((), ()))


def dot(a, b, dims=NN_DIMS):
    return lax.dot_general(a, b, dims, preferred_element_type=F32)


def iota(shape, dim):
    return lax.broadcasted_iota(jnp.int32, shape, dim)


def kernel(half, fe, ids, probs, grad, parked, wg, wu, wd, out,
           gbuf, pbuf, rx, rdy, tx, tdy, w0, wp, wf, acc, ps, pr, dbuf,
           sa_0, rta_0, rba_0, rla_0, rra_0, sa_1, rta_1, rba_1, rla_1, rra_1,
           sb_0, rtb_0, rbb_0, rlb_0, rrb_0, sb_1, rtb_1, rbb_1, rlb_1, rrb_1,
           sa2_0, ra2_0, sa2_1, ra2_1, sb2_0, rb2_0, sb2_1, rb2_1,
           t1, t1top, t1bottom, t1left, t1right, t2, t2r, acc_dh, send_sem, recv_sem, local_sem):
    piece = half // PIECES
    hc = half // 2
    core = lax.axis_index("swap")
    ep = lax.axis_index("ep")
    y = ep % NY
    z = (ep // NY) % NZ
    x = ep // (NY * NZ)

    def chip(dx, dy, dz):
        place = (((x + dx + NX) % NX) * NZ + (z + dz + NZ) % NZ) * NY + (y + dy + NY) % NY
        return (core, place)

    xp, xm = chip(1, 0, 0), chip(-1, 0, 0)
    yp, ym = chip(0, 1, 0), chip(0, -1, 0)
    zp, zm = chip(0, 0, 1), chip(0, 0, -1)
    xf, yf = chip(2, 0, 0), chip(0, 2, 0)
    a_refs = [(sa_0, rta_0, rba_0, rla_0, rra_0), (sa_1, rta_1, rba_1, rla_1, rra_1)]
    b_refs = [(sb_0, rtb_0, rbb_0, rlb_0, rrb_0), (sb_1, rtb_1, rbb_1, rlb_1, rrb_1)]
    sa2, ra2, sb2, rb2 = (sa2_0, sa2_1), (ra2_0, ra2_1), (sb2_0, sb2_1), (rb2_0, rb2_1)
    other = (1 - core, ep)

    copies, left_already = [], []

    def gone(copy):
        copy.wait_send()
        left_already.append(copy)

    def send(src, dst, device):
        k = len(copies)
        copy = pltpu.make_async_remote_copy(
            src_ref=src, dst_ref=dst, send_sem=send_sem.at[k], recv_sem=recv_sem.at[k],
            device_id=device, device_id_type=MESH)
        copies.append(copy)
        copy.start()
        return copy

    cols = pl.ds(pl.multiple_of(core * half, half), half)
    local = [
        pltpu.make_async_copy(parked.at[0], pbuf, local_sem.at[0]),
        pltpu.make_async_copy(grad.at[:, cols], gbuf, local_sem.at[1]),
        pltpu.make_async_copy(wg.at[:, cols], w0.at[0], local_sem.at[2]),
        pltpu.make_async_copy(wu.at[:, cols], w0.at[1], local_sem.at[3]),
        pltpu.make_async_copy(wd.at[:, cols], w0.at[2], local_sem.at[4]),
    ]
    barrier = pltpu.get_barrier_semaphore()
    for peer in (xp, xm, yp, ym, zp, zm, xf, yf, other):
        pl.semaphore_signal(barrier, inc=1, device_id=peer, device_id_type=MESH)
    for copy in local[2:] + local[:2]:
        copy.start()

    hits = ids[...] == fe[0]
    weight = jnp.sum(jnp.where(hits, probs[...], 0.0), axis=0, keepdims=True)
    flags = jnp.max(hits.astype(F32), axis=0, keepdims=True)
    before = (iota((TOK, TOK), 0) < iota((TOK, TOK), 1)).astype(F32).astype(BF16)
    ranks = dot(jnp.broadcast_to(flags, (16, TOK)).astype(BF16), before)[0:1]

    def match_of(slot, extra=None):
        rank_is = jnp.broadcast_to(ranks, slot.shape) == slot.astype(F32)
        m = jnp.where(rank_is, jnp.broadcast_to(flags, slot.shape), 0.0)
        if extra is not None:
            m = jnp.where(extra, m, 0.0)
        return m

    match_main = match_of(iota((MAIN, TOK), 0))
    tail_row = iota((16, TOK), 0)
    tail_slot = MAIN + tail_row % 2
    match_tail = match_of(tail_slot)
    pick = [match_of(tail_slot, tail_row // 2 == p).astype(BF16) for p in range(PIECES)]
    main16 = match_main.astype(BF16)

    def choose(src, rows, tails):
        rows[0:MAIN, :] = dot(main16, src[...]).astype(BF16)
        t = dot(pick[0], src[:, 0:piece])
        for p in range(1, PIECES):
            t = t + dot(pick[p], src[:, p * piece:(p + 1) * piece])
        tails[0:16, :] = t.astype(BF16)

    for copy in local[2:]:
        copy.wait()
    pl.semaphore_wait(barrier, 9)

    gu, dn = pl.ds(0, 2), pl.ds(2, 1)

    def ring(source, g, part, side):
        return send(source, wp.at[g, part, side], zp if side == 0 else zm)

    arrived = {}
    for part, name in ((gu, "gu"), (dn, "dn")):
        for side in (0, 1):
            arrived[0, name, side] = ring(w0.at[part], 0, part, side)

    def rows_of(s, n=1):
        return pl.ds(MAIN * s, MAIN * n)

    def tails_of(s, n=1):
        return pl.ds(16 * s, 16 * n)

    local[0].wait()
    choose(pbuf, rx, tx)
    px = [send(rx.at[rows_of(0)], rx.at[rows_of(3)], xp),
          send(rx.at[rows_of(0)], rx.at[rows_of(1)], xm),
          send(tx.at[tails_of(0)], tx.at[tails_of(3)], xp),
          send(tx.at[tails_of(0)], tx.at[tails_of(1)], xm)]
    local[1].wait()
    choose(gbuf, rdy, tdy)
    pd = [send(rdy.at[rows_of(0)], rdy.at[rows_of(12)], yp),
          send(rdy.at[rows_of(0)], rdy.at[rows_of(4)], ym),
          send(tdy.at[tails_of(0)], tdy.at[tails_of(12)], yp),
          send(tdy.at[tails_of(0)], tdy.at[tails_of(4)], ym)]

    def forward_rows(first, rows, tails, s3, s1, s2, plus, minus):
        for copy in first:
            copy.wait_recv()
        return [send(rows.at[pl.ds(MAIN * s3, 16)], rows.at[pl.ds(MAIN * s2, 16)], plus),
                send(rows.at[pl.ds(MAIN * s1 + 16, 16)], rows.at[pl.ds(MAIN * s2 + 16, 16)], minus),
                send(tails.at[tails_of(s1)], tails.at[tails_of(s2)], minus)]

    fx = forward_rows(px, rx, tx, 3, 1, 2, xp, xm)
    fd = forward_rows(pd, rdy, tdy, 12, 4, 8, yp, ym)
    for copy in fx:
        copy.wait_recv()
    px = [send(rx.at[rows_of(0, 4)], rx.at[rows_of(12, 4)], yp),
          send(rx.at[rows_of(0, 4)], rx.at[rows_of(4, 4)], ym),
          send(tx.at[tails_of(0, 4)], tx.at[tails_of(12, 4)], yp),
          send(tx.at[tails_of(0, 4)], tx.at[tails_of(4, 4)], ym)]
    for copy in fd:
        copy.wait_recv()
    pd_plus, pd_minus = [], []
    for j in range(4):
        pd_plus.append((send(rdy.at[rows_of(4 * j)], rdy.at[rows_of(4 * j + 3)], xp),
                        send(tdy.at[tails_of(4 * j)], tdy.at[tails_of(4 * j + 3)], xp)))
        pd_minus.append((send(rdy.at[rows_of(4 * j)], rdy.at[rows_of(4 * j + 1)], xm),
                         send(tdy.at[tails_of(4 * j)], tdy.at[tails_of(4 * j + 1)], xm)))

    def forward_weights(g, name, part):
        for side in (0, 1):
            arrived[g - 1, name, side].wait_recv()
            arrived[g, name, side] = ring(wp.at[g - 1, part, side], g, part, side)

    forward_weights(1, "gu", gu)

    for copy in px:
        copy.wait_recv()
    last = [send(rx.at[rows_of(12, 2)], rx.at[rows_of(8, 2)], yp),
            send(rx.at[rows_of(6, 2)], rx.at[rows_of(10, 2)], ym),
            send(tx.at[tails_of(12, 2)], tx.at[tails_of(8, 2)], yp),
            send(tx.at[tails_of(6, 2)], tx.at[tails_of(10, 2)], ym)]
    for pair in pd_plus + pd_minus:
        for copy in pair:
            copy.wait_recv()
    for j in range(4):
        s, to = (4 * j + 3, xp) if j < 2 else (4 * j + 1, xm)
        last.append(send(rdy.at[rows_of(s)], rdy.at[rows_of(4 * j + 2)], to))
        last.append(send(tdy.at[tails_of(s)], tdy.at[tails_of(4 * j + 2)], to))
    forward_weights(1, "dn", dn)
    for copy in last:
        copy.wait_recv()

    row, col = iota((MAIN, 256), 0), iota((MAIN, 256), 1)
    block = row // 2
    base = 16 * (4 * (block % 4) + block // 4) + row % 2
    for p in range(PIECES):
        e = jnp.where(col == base + 2 * p, 1.0, 0.0).astype(BF16)
        for tails, rows in ((tx, rx), (tdy, rdy)):
            rows[TAIL0:ROWS, p * piece:(p + 1) * piece] = dot(e, tails[...]).astype(BF16)

    def weights_of(g):
        if g == 0 or g == 4:
            w = w0 if g == 0 else wf
            return w[0:2].reshape(2 * FFD, half), w[2]
        return wp[g - 1, 0:2].reshape(4 * FFD, half), wp[g - 1, 2].reshape(2 * FFD, half)

    def width_of(g):
        return FFD if g in (0, 4) else 2 * FFD

    def partial_gate(g):
        wgu, _ = weights_of(g)

        @pl.loop(0, 2)
        def _(m):
            rows = pl.ds(pl.multiple_of(m * (ROWS // 2), 16), ROWS // 2)
            ps[g, rows, 0:2 * width_of(g)] = dot(rx[rows, :], wgu, NT_DIMS)

    def partial_dhid(g):
        _, wdn = weights_of(g)
        width = width_of(g)

        @pl.loop(0, 2)
        def _(m):
            rows = pl.ds(pl.multiple_of(m * (ROWS // 2), 16), ROWS // 2)
            dh = dot(rdy[rows, :], wdn, NT_DIMS)
            if width == FFD:
                dh = jnp.concatenate([dh, jnp.zeros_like(dh)], axis=1)
            ps[g, rows, 2 * width:2 * width + 128] = dh

    def exchange(g):
        used = pl.ds(0, 2 * width_of(g) + 128)
        return send(ps.at[g, :, used], pr.at[g, :, used], other)

    def finish(g, begun, lo=0, hi=ROWS // 32):
        for copy in begun:
            copy.wait_recv()
        width = width_of(g)

        @pl.loop(lo, hi)
        def _(m):
            rows = pl.ds(pl.multiple_of(m * 32, 32), 32)
            total = ps[g, rows, 0:2 * width + 128] + pr[g, rows, 0:2 * width + 128]
            gate, up = total[:, 0:width], total[:, width:2 * width]
            dhid = total[:, 2 * width:3 * width]
            s = 1.0 / (1.0 + jnp.exp(-gate))
            d_up = dhid * gate * s
            d_gate = dhid * up * s * (1.0 + gate * (1.0 - s))
            dbuf[rows, 0:2 * width] = jnp.concatenate([d_gate, d_up], axis=1).astype(BF16)

    tile = half // 6

    def back_tiles(g):
        width = width_of(g)

        @pl.loop(0, half // tile)
        def _(n):
            at = pl.ds(pl.multiple_of(n * tile, tile), tile)
            if g == 0:
                w = w0[0:2, :, at].reshape(2 * FFD, tile)
            else:
                w = wp[g - 1, 0:2, :, :, at].reshape(4 * FFD, tile)
            value = dot(dbuf[:, 0:2 * width], w)
            if g == 0:
                acc[:, at] = value
            else:
                acc[:, at] += value

    def begin(g):
        partial_gate(g)
        partial_dhid(g)
        return exchange(g)

    begun0, begun1 = begin(0), begin(1)
    forward_weights(2, "gu", gu)
    finish(0, [begun0])
    back_tiles(0)
    finish(1, [begun1])
    back_tiles(1)
    forward_weights(2, "dn", dn)
    begun2 = begin(2)
    finish(2, [begun2])
    back_tiles(2)

    before_far = len(copies)

    def forward_far(name, part):
        result = []
        for side in (0, 1):
            arrived[2, name, side].wait_recv()
            hid = pl.ds(32 * side, 32)
            to = zp if side == 0 else zm
            if name == "gu":
                result.append(send(wp.at[2, part, side, hid], wf.at[part, hid], to))
            else:
                result.append([send(wp.at[2, part, side, hid, pl.ds(lo, hc)], wf.at[part, hid, pl.ds(lo, hc)], to)
                               for lo in (0, hc)])
        return result

    far_gu = forward_far("gu", gu)
    partial_gate(3)
    far_dn = forward_far("dn", dn)
    partial_dhid(3)
    finish(3, [exchange(3)])
    back_tiles(3)
    for copy in far_gu:
        copy.wait_recv()
    partial_gate(4)
    far_gate = send(ps.at[4, :, pl.ds(0, 128)], pr.at[4, :, pl.ds(0, 128)], other)
    for copy in copies[:before_far]:
        gone(copy)
    before_sums = len(copies)
    for pair in far_dn:
        pair[0].wait_recv()
    acc_dh[...] = dot(rdy[:, 0:hc], wf[2, :, 0:hc], NT_DIMS)
    for pair in far_dn:
        pair[1].wait_recv()
    far_dhid = []
    for first, count in ((0, 288), (288, 256)):
        dh = acc_dh[first:first + count, :] + dot(rdy[first:first + count, hc:half], wf[2, :, hc:half], NT_DIMS)
        ps[4, first:first + count, 128:256] = jnp.concatenate([dh, jnp.zeros_like(dh)], axis=1)
        at = (4, pl.ds(first, count), pl.ds(128, 128))
        far_dhid.append(send(ps.at[at], pr.at[at], other))
    finish(4, [far_gate, far_dhid[0]], 0, 9)
    finish(4, [far_dhid[1]], 9, 17)

    def add(a, b):
        return (a.astype(F32) + b.astype(F32)).astype(BF16)

    def start_ring(ring):
        unit, top, bottom, left, right, plus, minus = ring
        up, down = pl.ds(0, 64), pl.ds(64, 64)
        return [send(unit.at[2, up], top, plus), send(unit.at[2, down], bottom, minus)]

    def rest_ring(ring):
        unit, top, bottom, left, right, plus, minus = ring
        up, down = pl.ds(0, 64), pl.ds(64, 64)
        return [send(unit.at[1, down], left.at[down], plus), send(unit.at[3, up], right.at[up], minus)]

    def turn_ring(begun, ends, ring):
        unit, top, bottom, left, right, plus, minus = ring
        up, down = pl.ds(0, 64), pl.ds(64, 64)
        begun[0].wait_recv()
        unit[1, up] = add(unit[1, up], top[...])
        ends.append(send(unit.at[1, up], left.at[up], plus))
        begun[1].wait_recv()
        unit[3, down] = add(unit[3, down], bottom[...])
        ends.append(send(unit.at[3, down], right.at[down], minus))

    def second(ends, ring, unit, arrivals, plus, minus, far):
        own, _, _, left, right, _, _ = ring
        for copy in ends:
            copy.wait_recv()
        for k in (2, 1, 3, 0):
            rows = slice(32 * k, 32 * k + 32)
            unit[k] = (own[0, rows].astype(F32) + left[rows].astype(F32) + right[rows].astype(F32)).astype(BF16)
        return scatter(unit, arrivals, plus, minus, far)

    def scatter(unit, arrivals, plus, minus, far):
        return [send(unit.at[2], arrivals.at[1], far),
                send(unit.at[1], arrivals.at[0], plus), send(unit.at[3], arrivals.at[2], minus)]

    rings_a = [a + (xp, xm) for a in a_refs]
    rings_b = [b + (yp, ym) for b in b_refs]

    def last_tiles(c, is_a):
        n0, n1 = (0, 3) if c == 0 else (3, 4)
        for n in range(n0, n1):
            p = n if is_a else n + 4
            at = slice(p * piece, (p + 1) * piece)
            to = slice((n - n0) * piece, (n - n0 + 1) * piece)
            value = acc[0:TAIL0, at] + dot(dbuf[0:TAIL0, 0:2 * FFD], wf[0:2, :, at].reshape(2 * FFD, piece))
            for i in range(4):
                for j in range(4):
                    s = 4 * j + i
                    block = value[MAIN * s:MAIN * s + MAIN].astype(BF16)
                    if is_a:
                        rings_a[c][0][i, 32 * j:32 * j + 32, to] = block
                    else:
                        rings_b[c][0][j, 32 * i:32 * i + 32, to] = block

    begun_a, begun_b, ends_a, ends_b = [], [], [], []
    last_tiles(0, False)
    begun_b.append(start_ring(rings_b[0]))
    last_tiles(0, True)
    begun_a.append(start_ring(rings_a[0]))

    low_half, high_half = pl.ds(0, hc // 2), pl.ds(hc // 2, hc // 2)
    tails = acc[TAIL0:ROWS, :] + dot(dbuf[TAIL0:ROWS, 0:2 * FFD], wf[0:2].reshape(2 * FFD, half))
    for i in range(4):
        t = tails[8 * i:8 * i + 8, :]
        t1[i] = jnp.concatenate([t[:, 0:hc], t[:, hc:half]], axis=0).astype(BF16)
    tail_top = send(t1.at[2, :, low_half], t1top, xp)
    tail_bottom = send(t1.at[2, :, high_half], t1bottom, xm)

    last_tiles(1, False)
    begun_b.append(start_ring(rings_b[1]))
    last_tiles(1, True)
    begun_a.append(start_ring(rings_a[1]))

    tail_ends = [send(t1.at[1, :, high_half], t1left.at[:, high_half], xp),
                 send(t1.at[3, :, low_half], t1right.at[:, low_half], xm)]
    for copy in begun_b[0] + begun_a[0]:
        gone(copy)
    ends_b.append(rest_ring(rings_b[0]))
    ends_a.append(rest_ring(rings_a[0]))
    tail_top.wait_recv()
    t1[1, :, low_half] = add(t1[1, :, low_half], t1top[...])
    tail_ends.append(send(t1.at[1, :, low_half], t1left.at[:, low_half], xp))
    tail_bottom.wait_recv()
    t1[3, :, high_half] = add(t1[3, :, high_half], t1bottom[...])
    tail_ends.append(send(t1.at[3, :, high_half], t1right.at[:, high_half], xm))
    turn_ring(begun_b[0], ends_b[0], rings_b[0])
    turn_ring(begun_a[0], ends_a[0], rings_a[0])
    ends_b.append(rest_ring(rings_b[1]))
    ends_a.append(rest_ring(rings_a[1]))
    turn_ring(begun_b[1], ends_b[1], rings_b[1])
    turn_ring(begun_a[1], ends_a[1], rings_a[1])

    for copy in tail_ends:
        copy.wait_recv()
    tail = (t1[0].astype(F32) + t1left[...].astype(F32) + t1right[...].astype(F32)).astype(BF16)
    row, col = iota((64, 16), 0), iota((64, 16), 1)
    p_of = (row % 16) // 2
    wanted = 8 * (p_of // 4) + 2 * (row // 16) + row % 2
    packed = jnp.zeros((64, piece), F32)
    for q in range(4):
        f = jnp.where((col == wanted) & (p_of % 4 == q), 1.0, 0.0).astype(BF16)
        packed = packed + dot(f, tail[:, q * piece:(q + 1) * piece])
    t2[...] = packed.astype(BF16).reshape(4, 16, piece)
    tail_ends = scatter(t2, t2r, yp, ym, yf)

    before_second = len(copies)
    last_b, last_a = [], []
    for c in range(2):
        last_b.append(second(ends_b[c], rings_b[c], sb2[c], rb2[c], xp, xm, xf))
        last_a.append(second(ends_a[c], rings_a[c], sa2[c], ra2[c], yp, ym, yf))

    for copy in copies[before_sums:before_second]:
        if not any(copy is other_copy for other_copy in left_already):
            gone(copy)
    slot_weight = 0.5 * jnp.sum(match_main * weight, axis=1, keepdims=True)
    tail_weight = 0.5 * jnp.sum(match_tail * weight, axis=1, keepdims=True)

    def total(unit, arrivals, at=None):
        if at is None:
            return unit[0].astype(F32) + arrivals[0].astype(F32) + arrivals[1].astype(F32) + arrivals[2].astype(F32)
        return (unit[0, :, at].astype(F32) + arrivals[0, :, at].astype(F32)
                + arrivals[1, :, at].astype(F32) + arrivals[2, :, at].astype(F32))

    for copy in tail_ends:
        copy.wait_recv()
    tail = total(t2, t2r) * tail_weight
    for c in range(2):
        for ends, unit, arrivals, p0 in ((last_b[c], sb2[c], rb2[c], 4), (last_a[c], sa2[c], ra2[c], 0)):
            for copy in ends:
                copy.wait_recv()
            n0, n1 = (0, 3) if c == 0 else (3, 4)
            for n in range(n0, n1):
                p = p0 + n
                at = slice(p * piece, (p + 1) * piece)
                q = slice((n - n0) * piece, (n - n0 + 1) * piece)
                value = jnp.concatenate([total(unit, arrivals, q) * slot_weight, tail], axis=0)
                high = value.astype(BF16)
                low = (value - high.astype(F32)).astype(BF16)
                m = jnp.concatenate([main16, pick[p]], axis=0)
                spread = dot(m, high, TN_DIMS) + dot(m, low, TN_DIMS)
                out[:, at] = (gbuf[:, at].astype(F32) + spread).astype(BF16)

    for copy in copies:
        if not any(copy is other_copy for other_copy in left_already):
            copy.wait_send()


def solution(mesh):
    def on_device(grad_out, parked_inputs, route_ids, route_probs, flight_expert, w_gate, w_up, w_down):
        features = grad_out.shape[1]
        half = features // 2
        hc, piece = half // 2, half // PIECES
        vmem = pltpu.VMEM
        ring_scratch, second_scratch = [], []
        for _ in range(2):
            for width in (3 * piece, piece):
                ring_scratch += [vmem((4, 128, width), BF16), vmem((64, width), BF16), vmem((64, width), BF16),
                                 vmem((128, width), BF16), vmem((128, width), BF16)]
                second_scratch += [vmem((4, 32, width), BF16), vmem((3, 32, width), BF16)]
        scratch = [
            vmem((TOK, half), BF16), vmem((TOK, half), BF16),
            vmem((ROWS, half), BF16), vmem((ROWS, half), BF16),
            vmem((256, piece), BF16), vmem((256, piece), BF16),
            vmem((3, FFD, half), BF16), vmem((3, 3, 2, FFD, half), BF16), vmem((3, FFD, half), BF16),
            vmem((ROWS, half), F32),
            vmem((5, ROWS, 384), F32), vmem((5, ROWS, 384), F32),
            vmem((ROWS, 256), BF16),
            *ring_scratch, *second_scratch,
            vmem((4, 16, hc), BF16), vmem((16, hc // 2), BF16), vmem((16, hc // 2), BF16),
            vmem((16, hc), BF16), vmem((16, hc), BF16),
            vmem((4, 16, piece), BF16), vmem((3, 16, piece), BF16),
            vmem((ROWS, FFD), F32),
            pltpu.SemaphoreType.DMA((NUM_SEMS,)), pltpu.SemaphoreType.DMA((NUM_SEMS,)),
            pltpu.SemaphoreType.DMA((5,)),
        ]
        any_space = pl.BlockSpec(memory_space=pl.ANY)
        in_vmem = pl.BlockSpec(memory_space=pltpu.VMEM)

        def body(*refs):
            kernel(half, *refs)

        return pl.pallas_call(
            body,
            out_shape=jax.ShapeDtypeStruct((TOK, half), BF16),
            in_specs=[pl.BlockSpec(memory_space=pltpu.SMEM), in_vmem, in_vmem,
                      any_space, any_space, any_space, any_space, any_space],
            out_specs=in_vmem,
            scratch_shapes=scratch,
            compiler_params=pltpu.CompilerParams(
                collective_id=0, has_side_effects=True, vmem_limit_bytes=60 * 1024 * 1024),
            cost_estimate=pl.CostEstimate(
                flops=10 * ROWS * 8 * FFD * half, bytes_accessed=10_000_000, transcendentals=ROWS * 512),
            name="routed_swiglu_backward",
        )(flight_expert, route_ids.T, route_probs.T, grad_out, parked_inputs, w_gate.T, w_up.T, w_down)

    in_specs = (
        P("ep", None),
        P("swap", "ep", None),
        P("ep", None),
        P("ep", None),
        P(),
        P(None, "ep"),
        P(None, "ep"),
        P("ep", None),
    )
    return jax.shard_map(
        on_device, mesh=mesh, in_specs=in_specs, out_specs=P("ep", "swap"), check_vma=False
    )
```

```python
import jax
import jax.numpy as jnp
from jax import lax
from jax.experimental import pallas as pl
from jax.experimental.pallas import tpu as pltpu
from jax.sharding import PartitionSpec as P

MESH = pl.DeviceIdType.MESH
BF16 = jnp.bfloat16
F32 = jnp.float32

CAP = 34
TOK = 128
FFD = 64
NX, NY, NZ = 4, 4, 8
MAIN = 32
ROWS = 16 * CAP
TAIL0 = 16 * MAIN
PIECES = 8
NUM_SEMS = 128
NT_DIMS = (((1,), (1,)), ((), ()))
NN_DIMS = (((1,), (0,)), ((), ()))
TN_DIMS = (((0,), (0,)), ((), ()))


def dot(a, b, dims=NN_DIMS):
    return lax.dot_general(a, b, dims, preferred_element_type=F32)


def iota(shape, dim):
    return lax.broadcasted_iota(jnp.int32, shape, dim)


def kernel(half, fe, ids, probs, grad, parked, wg, wu, wd, out,
           gbuf, pbuf, rx, rdy, tx, tdy, w0, wp, wf, acc, ps, pr, dbuf,
           sa_0, rta_0, rba_0, rla_0, rra_0, sa_1, rta_1, rba_1, rla_1, rra_1,
           sb_0, rtb_0, rbb_0, rlb_0, rrb_0, sb_1, rtb_1, rbb_1, rlb_1, rrb_1,
           sa2_0, ra2_0, sa2_1, ra2_1, sb2_0, rb2_0, sb2_1, rb2_1,
           t1, t1top, t1bottom, t1left, t1right, t2, t2r, acc_dh, send_sem, recv_sem, local_sem):
    piece = half // PIECES
    hc = half // 2
    core = lax.axis_index("swap")
    ep = lax.axis_index("ep")
    y = ep % NY
    z = (ep // NY) % NZ
    x = ep // (NY * NZ)

    def chip(dx, dy, dz):
        place = (((x + dx + NX) % NX) * NZ + (z + dz + NZ) % NZ) * NY + (y + dy + NY) % NY
        return (core, place)

    xp, xm = chip(1, 0, 0), chip(-1, 0, 0)
    yp, ym = chip(0, 1, 0), chip(0, -1, 0)
    zp, zm = chip(0, 0, 1), chip(0, 0, -1)
    xf, yf = chip(2, 0, 0), chip(0, 2, 0)
    a_refs = [(sa_0, rta_0, rba_0, rla_0, rra_0), (sa_1, rta_1, rba_1, rla_1, rra_1)]
    b_refs = [(sb_0, rtb_0, rbb_0, rlb_0, rrb_0), (sb_1, rtb_1, rbb_1, rlb_1, rrb_1)]
    sa2, ra2, sb2, rb2 = (sa2_0, sa2_1), (ra2_0, ra2_1), (sb2_0, sb2_1), (rb2_0, rb2_1)
    other = (1 - core, ep)

    copies, left_already = [], []

    def gone(copy):
        copy.wait_send()
        left_already.append(copy)

    def send(src, dst, device):
        k = len(copies)
        copy = pltpu.make_async_remote_copy(
            src_ref=src, dst_ref=dst, send_sem=send_sem.at[k], recv_sem=recv_sem.at[k],
            device_id=device, device_id_type=MESH)
        copies.append(copy)
        copy.start()
        return copy

    cols = pl.ds(pl.multiple_of(core * half, half), half)
    local = [
        pltpu.make_async_copy(parked.at[0], pbuf, local_sem.at[0]),
        pltpu.make_async_copy(grad.at[:, cols], gbuf, local_sem.at[1]),
        pltpu.make_async_copy(wg.at[:, cols], w0.at[0], local_sem.at[2]),
        pltpu.make_async_copy(wu.at[:, cols], w0.at[1], local_sem.at[3]),
        pltpu.make_async_copy(wd.at[:, cols], w0.at[2], local_sem.at[4]),
    ]
    barrier = pltpu.get_barrier_semaphore()
    for peer in (xp, xm, yp, ym, zp, zm, xf, yf, other):
        pl.semaphore_signal(barrier, inc=1, device_id=peer, device_id_type=MESH)
    for copy in local[2:] + local[:2]:
        copy.start()

    hits = ids[...] == fe[0]
    weight = jnp.sum(jnp.where(hits, probs[...], 0.0), axis=0, keepdims=True)
    flags = jnp.max(hits.astype(F32), axis=0, keepdims=True)
    before = (iota((TOK, TOK), 0) < iota((TOK, TOK), 1)).astype(F32).astype(BF16)
    ranks = dot(jnp.broadcast_to(flags, (16, TOK)).astype(BF16), before)[0:1]

    def match_of(slot, extra=None):
        rank_is = jnp.broadcast_to(ranks, slot.shape) == slot.astype(F32)
        m = jnp.where(rank_is, jnp.broadcast_to(flags, slot.shape), 0.0)
        if extra is not None:
            m = jnp.where(extra, m, 0.0)
        return m

    match_main = match_of(iota((MAIN, TOK), 0))
    tail_row = iota((16, TOK), 0)
    tail_slot = MAIN + tail_row % 2
    match_tail = match_of(tail_slot)
    pick = [match_of(tail_slot, tail_row // 2 == p).astype(BF16) for p in range(PIECES)]
    main16 = match_main.astype(BF16)

    def choose(src, rows, tails):
        rows[0:MAIN, :] = dot(main16, src[...]).astype(BF16)
        t = dot(pick[0], src[:, 0:piece])
        for p in range(1, PIECES):
            t = t + dot(pick[p], src[:, p * piece:(p + 1) * piece])
        tails[0:16, :] = t.astype(BF16)

    for copy in local[2:]:
        copy.wait()
    pl.semaphore_wait(barrier, 9)

    gu, dn = pl.ds(0, 2), pl.ds(2, 1)

    def ring(source, g, part, side):
        return send(source, wp.at[g, part, side], zp if side == 0 else zm)

    arrived = {}
    for part, name in ((gu, "gu"), (dn, "dn")):
        for side in (0, 1):
            arrived[0, name, side] = ring(w0.at[part], 0, part, side)

    def rows_of(s, n=1):
        return pl.ds(MAIN * s, MAIN * n)

    def tails_of(s, n=1):
        return pl.ds(16 * s, 16 * n)

    local[0].wait()
    choose(pbuf, rx, tx)
    px = [send(rx.at[rows_of(0)], rx.at[rows_of(3)], xp),
          send(rx.at[rows_of(0)], rx.at[rows_of(1)], xm),
          send(tx.at[tails_of(0)], tx.at[tails_of(3)], xp),
          send(tx.at[tails_of(0)], tx.at[tails_of(1)], xm)]
    local[1].wait()
    choose(gbuf, rdy, tdy)
    pd = [send(rdy.at[rows_of(0)], rdy.at[rows_of(12)], yp),
          send(rdy.at[rows_of(0)], rdy.at[rows_of(4)], ym),
          send(tdy.at[tails_of(0)], tdy.at[tails_of(12)], yp),
          send(tdy.at[tails_of(0)], tdy.at[tails_of(4)], ym)]

    def forward_rows(first, rows, tails, s3, s1, s2, plus, minus):
        for copy in first:
            copy.wait_recv()
        return [send(rows.at[pl.ds(MAIN * s3, 16)], rows.at[pl.ds(MAIN * s2, 16)], plus),
                send(rows.at[pl.ds(MAIN * s1 + 16, 16)], rows.at[pl.ds(MAIN * s2 + 16, 16)], minus),
                send(tails.at[tails_of(s1)], tails.at[tails_of(s2)], minus)]

    fx = forward_rows(px, rx, tx, 3, 1, 2, xp, xm)
    fd = forward_rows(pd, rdy, tdy, 12, 4, 8, yp, ym)
    for copy in fx:
        copy.wait_recv()
    px = [send(rx.at[rows_of(0, 4)], rx.at[rows_of(12, 4)], yp),
          send(rx.at[rows_of(0, 4)], rx.at[rows_of(4, 4)], ym),
          send(tx.at[tails_of(0, 4)], tx.at[tails_of(12, 4)], yp),
          send(tx.at[tails_of(0, 4)], tx.at[tails_of(4, 4)], ym)]
    for copy in fd:
        copy.wait_recv()
    pd_plus, pd_minus = [], []
    for j in range(4):
        pd_plus.append((send(rdy.at[rows_of(4 * j)], rdy.at[rows_of(4 * j + 3)], xp),
                        send(tdy.at[tails_of(4 * j)], tdy.at[tails_of(4 * j + 3)], xp)))
        pd_minus.append((send(rdy.at[rows_of(4 * j)], rdy.at[rows_of(4 * j + 1)], xm),
                         send(tdy.at[tails_of(4 * j)], tdy.at[tails_of(4 * j + 1)], xm)))

    def forward_weights(g, name, part):
        for side in (0, 1):
            arrived[g - 1, name, side].wait_recv()
            arrived[g, name, side] = ring(wp.at[g - 1, part, side], g, part, side)

    forward_weights(1, "gu", gu)

    for copy in px:
        copy.wait_recv()
    last = [send(rx.at[rows_of(12, 2)], rx.at[rows_of(8, 2)], yp),
            send(rx.at[rows_of(6, 2)], rx.at[rows_of(10, 2)], ym),
            send(tx.at[tails_of(12, 2)], tx.at[tails_of(8, 2)], yp),
            send(tx.at[tails_of(6, 2)], tx.at[tails_of(10, 2)], ym)]
    for pair in pd_plus + pd_minus:
        for copy in pair:
            copy.wait_recv()
    for j in range(4):
        s, to = (4 * j + 3, xp) if j < 2 else (4 * j + 1, xm)
        last.append(send(rdy.at[rows_of(s)], rdy.at[rows_of(4 * j + 2)], to))
        last.append(send(tdy.at[tails_of(s)], tdy.at[tails_of(4 * j + 2)], to))
    forward_weights(1, "dn", dn)
    for copy in last:
        copy.wait_recv()

    row, col = iota((MAIN, 256), 0), iota((MAIN, 256), 1)
    block = row // 2
    base = 16 * (4 * (block % 4) + block // 4) + row % 2
    for p in range(PIECES):
        e = jnp.where(col == base + 2 * p, 1.0, 0.0).astype(BF16)
        for tails, rows in ((tx, rx), (tdy, rdy)):
            rows[TAIL0:ROWS, p * piece:(p + 1) * piece] = dot(e, tails[...]).astype(BF16)

    def weights_of(g):
        if g == 0 or g == 4:
            w = w0 if g == 0 else wf
            return w[0:2].reshape(2 * FFD, half), w[2]
        return wp[g - 1, 0:2].reshape(4 * FFD, half), wp[g - 1, 2].reshape(2 * FFD, half)

    def width_of(g):
        return FFD if g in (0, 4) else 2 * FFD

    def partial_gate(g):
        wgu, _ = weights_of(g)

        @pl.loop(0, 2)
        def _(m):
            rows = pl.ds(pl.multiple_of(m * (ROWS // 2), 16), ROWS // 2)
            ps[g, rows, 0:2 * width_of(g)] = dot(rx[rows, :], wgu, NT_DIMS)

    def partial_dhid(g):
        _, wdn = weights_of(g)
        width = width_of(g)

        @pl.loop(0, 2)
        def _(m):
            rows = pl.ds(pl.multiple_of(m * (ROWS // 2), 16), ROWS // 2)
            dh = dot(rdy[rows, :], wdn, NT_DIMS)
            if width == FFD:
                dh = jnp.concatenate([dh, jnp.zeros_like(dh)], axis=1)
            ps[g, rows, 2 * width:2 * width + 128] = dh

    def exchange(g):
        used = pl.ds(0, 2 * width_of(g) + 128)
        return send(ps.at[g, :, used], pr.at[g, :, used], other)

    def finish(g, begun, lo=0, hi=ROWS // 32):
        for copy in begun:
            copy.wait_recv()
        width = width_of(g)

        @pl.loop(lo, hi)
        def _(m):
            rows = pl.ds(pl.multiple_of(m * 32, 32), 32)
            total = ps[g, rows, 0:2 * width + 128] + pr[g, rows, 0:2 * width + 128]
            gate, up = total[:, 0:width], total[:, width:2 * width]
            dhid = total[:, 2 * width:3 * width]
            s = 1.0 / (1.0 + jnp.exp(-gate))
            d_up = dhid * gate * s
            d_gate = dhid * up * s * (1.0 + gate * (1.0 - s))
            dbuf[rows, 0:2 * width] = jnp.concatenate([d_gate, d_up], axis=1).astype(BF16)

    tile = half // 6

    def back_tiles(g):
        width = width_of(g)

        @pl.loop(0, half // tile)
        def _(n):
            at = pl.ds(pl.multiple_of(n * tile, tile), tile)
            if g == 0:
                w = w0[0:2, :, at].reshape(2 * FFD, tile)
            else:
                w = wp[g - 1, 0:2, :, :, at].reshape(4 * FFD, tile)
            value = dot(dbuf[:, 0:2 * width], w)
            if g == 0:
                acc[:, at] = value
            else:
                acc[:, at] += value

    def begin(g):
        partial_gate(g)
        partial_dhid(g)
        return exchange(g)

    begun0, begun1 = begin(0), begin(1)
    forward_weights(2, "gu", gu)
    finish(0, [begun0])
    back_tiles(0)
    finish(1, [begun1])
    back_tiles(1)
    forward_weights(2, "dn", dn)
    begun2 = begin(2)
    finish(2, [begun2])
    back_tiles(2)

    before_far = len(copies)

    def forward_far(name, part):
        result = []
        for side in (0, 1):
            arrived[2, name, side].wait_recv()
            hid = pl.ds(32 * side, 32)
            to = zp if side == 0 else zm
            if name == "gu":
                result.append(send(wp.at[2, part, side, hid], wf.at[part, hid], to))
            else:
                result.append([send(wp.at[2, part, side, hid, pl.ds(lo, hc)], wf.at[part, hid, pl.ds(lo, hc)], to)
                               for lo in (0, hc)])
        return result

    far_gu = forward_far("gu", gu)
    partial_gate(3)
    far_dn = forward_far("dn", dn)
    partial_dhid(3)
    finish(3, [exchange(3)])
    back_tiles(3)
    for copy in far_gu:
        copy.wait_recv()
    partial_gate(4)
    far_gate = send(ps.at[4, :, pl.ds(0, 128)], pr.at[4, :, pl.ds(0, 128)], other)
    for copy in copies[:before_far]:
        gone(copy)
    before_sums = len(copies)
    for pair in far_dn:
        pair[0].wait_recv()
    acc_dh[...] = dot(rdy[:, 0:hc], wf[2, :, 0:hc], NT_DIMS)
    for pair in far_dn:
        pair[1].wait_recv()
    far_dhid = []
    for first, count in ((0, 288), (288, 256)):
        dh = acc_dh[first:first + count, :] + dot(rdy[first:first + count, hc:half], wf[2, :, hc:half], NT_DIMS)
        ps[4, first:first + count, 128:256] = jnp.concatenate([dh, jnp.zeros_like(dh)], axis=1)
        at = (4, pl.ds(first, count), pl.ds(128, 128))
        far_dhid.append(send(ps.at[at], pr.at[at], other))
    finish(4, [far_gate, far_dhid[0]], 0, 9)
    finish(4, [far_dhid[1]], 9, 17)

    def add(a, b):
        return (a.astype(F32) + b.astype(F32)).astype(BF16)

    def start_ring(ring):
        unit, top, bottom, left, right, plus, minus = ring
        up, down = pl.ds(0, 64), pl.ds(64, 64)
        return [send(unit.at[2, up], top, plus), send(unit.at[2, down], bottom, minus)]

    def rest_ring(ring):
        unit, top, bottom, left, right, plus, minus = ring
        up, down = pl.ds(0, 64), pl.ds(64, 64)
        return [send(unit.at[1, down], left.at[down], plus), send(unit.at[3, up], right.at[up], minus)]

    def turn_ring(begun, ends, ring):
        unit, top, bottom, left, right, plus, minus = ring
        up, down = pl.ds(0, 64), pl.ds(64, 64)
        begun[0].wait_recv()
        unit[1, up] = add(unit[1, up], top[...])
        ends.append(send(unit.at[1, up], left.at[up], plus))
        begun[1].wait_recv()
        unit[3, down] = add(unit[3, down], bottom[...])
        ends.append(send(unit.at[3, down], right.at[down], minus))

    def second(ends, ring, unit, arrivals, plus, minus, far):
        own, _, _, left, right, _, _ = ring
        for copy in ends:
            copy.wait_recv()
        for k in (2, 1, 3, 0):
            rows = slice(32 * k, 32 * k + 32)
            unit[k] = (own[0, rows].astype(F32) + left[rows].astype(F32) + right[rows].astype(F32)).astype(BF16)
        return scatter(unit, arrivals, plus, minus, far)

    def scatter(unit, arrivals, plus, minus, far):
        return [send(unit.at[2], arrivals.at[1], far),
                send(unit.at[1], arrivals.at[0], plus), send(unit.at[3], arrivals.at[2], minus)]

    rings_a = [a + (xp, xm) for a in a_refs]
    rings_b = [b + (yp, ym) for b in b_refs]

    def last_tiles(c, is_a):
        n0, n1 = (0, 3) if c == 0 else (3, 4)
        for n in range(n0, n1):
            p = n if is_a else n + 4
            at = slice(p * piece, (p + 1) * piece)
            to = slice((n - n0) * piece, (n - n0 + 1) * piece)
            value = acc[0:TAIL0, at] + dot(dbuf[0:TAIL0, 0:2 * FFD], wf[0:2, :, at].reshape(2 * FFD, piece))
            for i in range(4):
                for j in range(4):
                    s = 4 * j + i
                    block = value[MAIN * s:MAIN * s + MAIN].astype(BF16)
                    if is_a:
                        rings_a[c][0][i, 32 * j:32 * j + 32, to] = block
                    else:
                        rings_b[c][0][j, 32 * i:32 * i + 32, to] = block

    begun_a, begun_b, ends_a, ends_b = [], [], [], []
    last_tiles(0, True)
    begun_a.append(start_ring(rings_a[0]))
    last_tiles(0, False)
    begun_b.append(start_ring(rings_b[0]))

    low_half, high_half = pl.ds(0, hc // 2), pl.ds(hc // 2, hc // 2)
    tails = acc[TAIL0:ROWS, :] + dot(dbuf[TAIL0:ROWS, 0:2 * FFD], wf[0:2].reshape(2 * FFD, half))
    for i in range(4):
        t = tails[8 * i:8 * i + 8, :]
        t1[i] = jnp.concatenate([t[:, 0:hc], t[:, hc:half]], axis=0).astype(BF16)
    tail_top = send(t1.at[2, :, low_half], t1top, xp)
    tail_bottom = send(t1.at[2, :, high_half], t1bottom, xm)

    last_tiles(1, True)
    begun_a.append(start_ring(rings_a[1]))
    last_tiles(1, False)
    begun_b.append(start_ring(rings_b[1]))

    tail_ends = [send(t1.at[1, :, high_half], t1left.at[:, high_half], xp),
                 send(t1.at[3, :, low_half], t1right.at[:, low_half], xm)]
    for copy in begun_b[0] + begun_a[0]:
        gone(copy)
    ends_a.append(rest_ring(rings_a[0]))
    ends_b.append(rest_ring(rings_b[0]))
    tail_top.wait_recv()
    t1[1, :, low_half] = add(t1[1, :, low_half], t1top[...])
    tail_ends.append(send(t1.at[1, :, low_half], t1left.at[:, low_half], xp))
    tail_bottom.wait_recv()
    t1[3, :, high_half] = add(t1[3, :, high_half], t1bottom[...])
    tail_ends.append(send(t1.at[3, :, high_half], t1right.at[:, high_half], xm))
    turn_ring(begun_a[0], ends_a[0], rings_a[0])
    turn_ring(begun_b[0], ends_b[0], rings_b[0])
    ends_a.append(rest_ring(rings_a[1]))
    ends_b.append(rest_ring(rings_b[1]))
    turn_ring(begun_a[1], ends_a[1], rings_a[1])
    turn_ring(begun_b[1], ends_b[1], rings_b[1])

    for copy in tail_ends:
        copy.wait_recv()
    tail = (t1[0].astype(F32) + t1left[...].astype(F32) + t1right[...].astype(F32)).astype(BF16)
    row, col = iota((64, 16), 0), iota((64, 16), 1)
    p_of = (row % 16) // 2
    wanted = 8 * (p_of // 4) + 2 * (row // 16) + row % 2
    packed = jnp.zeros((64, piece), F32)
    for q in range(4):
        f = jnp.where((col == wanted) & (p_of % 4 == q), 1.0, 0.0).astype(BF16)
        packed = packed + dot(f, tail[:, q * piece:(q + 1) * piece])
    t2[...] = packed.astype(BF16).reshape(4, 16, piece)
    tail_ends = scatter(t2, t2r, yp, ym, yf)

    before_second = len(copies)
    last_b, last_a = [], []
    for c in range(2):
        last_b.append(second(ends_b[c], rings_b[c], sb2[c], rb2[c], xp, xm, xf))
        last_a.append(second(ends_a[c], rings_a[c], sa2[c], ra2[c], yp, ym, yf))

    for copy in copies[before_sums:before_second]:
        if not any(copy is other_copy for other_copy in left_already):
            gone(copy)
    slot_weight = 0.5 * jnp.sum(match_main * weight, axis=1, keepdims=True)
    tail_weight = 0.5 * jnp.sum(match_tail * weight, axis=1, keepdims=True)

    def total(unit, arrivals, at=None):
        if at is None:
            return unit[0].astype(F32) + arrivals[0].astype(F32) + arrivals[1].astype(F32) + arrivals[2].astype(F32)
        return (unit[0, :, at].astype(F32) + arrivals[0, :, at].astype(F32)
                + arrivals[1, :, at].astype(F32) + arrivals[2, :, at].astype(F32))

    for copy in tail_ends:
        copy.wait_recv()
    tail = total(t2, t2r) * tail_weight
    for c in range(2):
        for ends, unit, arrivals, p0 in ((last_b[c], sb2[c], rb2[c], 4), (last_a[c], sa2[c], ra2[c], 0)):
            for copy in ends:
                copy.wait_recv()
            n0, n1 = (0, 3) if c == 0 else (3, 4)
            for n in range(n0, n1):
                p = p0 + n
                at = slice(p * piece, (p + 1) * piece)
                q = slice((n - n0) * piece, (n - n0 + 1) * piece)
                value = jnp.concatenate([total(unit, arrivals, q) * slot_weight, tail], axis=0)
                high = value.astype(BF16)
                low = (value - high.astype(F32)).astype(BF16)
                m = jnp.concatenate([main16, pick[p]], axis=0)
                spread = dot(m, high, TN_DIMS) + dot(m, low, TN_DIMS)
                out[:, at] = (gbuf[:, at].astype(F32) + spread).astype(BF16)

    for copy in copies:
        if not any(copy is other_copy for other_copy in left_already):
            copy.wait_send()


def solution(mesh):
    def on_device(grad_out, parked_inputs, route_ids, route_probs, flight_expert, w_gate, w_up, w_down):
        features = grad_out.shape[1]
        half = features // 2
        hc, piece = half // 2, half // PIECES
        vmem = pltpu.VMEM
        ring_scratch, second_scratch = [], []
        for _ in range(2):
            for width in (3 * piece, piece):
                ring_scratch += [vmem((4, 128, width), BF16), vmem((64, width), BF16), vmem((64, width), BF16),
                                 vmem((128, width), BF16), vmem((128, width), BF16)]
                second_scratch += [vmem((4, 32, width), BF16), vmem((3, 32, width), BF16)]
        scratch = [
            vmem((TOK, half), BF16), vmem((TOK, half), BF16),
            vmem((ROWS, half), BF16), vmem((ROWS, half), BF16),
            vmem((256, piece), BF16), vmem((256, piece), BF16),
            vmem((3, FFD, half), BF16), vmem((3, 3, 2, FFD, half), BF16), vmem((3, FFD, half), BF16),
            vmem((ROWS, half), F32),
            vmem((5, ROWS, 384), F32), vmem((5, ROWS, 384), F32),
            vmem((ROWS, 256), BF16),
            *ring_scratch, *second_scratch,
            vmem((4, 16, hc), BF16), vmem((16, hc // 2), BF16), vmem((16, hc // 2), BF16),
            vmem((16, hc), BF16), vmem((16, hc), BF16),
            vmem((4, 16, piece), BF16), vmem((3, 16, piece), BF16),
            vmem((ROWS, FFD), F32),
            pltpu.SemaphoreType.DMA((NUM_SEMS,)), pltpu.SemaphoreType.DMA((NUM_SEMS,)),
            pltpu.SemaphoreType.DMA((5,)),
        ]
        any_space = pl.BlockSpec(memory_space=pl.ANY)
        in_vmem = pl.BlockSpec(memory_space=pltpu.VMEM)

        def body(*refs):
            kernel(half, *refs)

        return pl.pallas_call(
            body,
            out_shape=jax.ShapeDtypeStruct((TOK, half), BF16),
            in_specs=[pl.BlockSpec(memory_space=pltpu.SMEM), in_vmem, in_vmem,
                      any_space, any_space, any_space, any_space, any_space],
            out_specs=in_vmem,
            scratch_shapes=scratch,
            compiler_params=pltpu.CompilerParams(
                collective_id=0, has_side_effects=True, vmem_limit_bytes=60 * 1024 * 1024),
            cost_estimate=pl.CostEstimate(
                flops=10 * ROWS * 8 * FFD * half, bytes_accessed=10_000_000, transcendentals=ROWS * 512),
            name="routed_swiglu_backward",
        )(flight_expert, route_ids.T, route_probs.T, grad_out, parked_inputs, w_gate.T, w_up.T, w_down)

    in_specs = (
        P("ep", None),
        P("swap", "ep", None),
        P("ep", None),
        P("ep", None),
        P(),
        P(None, "ep"),
        P(None, "ep"),
        P("ep", None),
    )
    return jax.shard_map(
        on_device, mesh=mesh, in_specs=in_specs, out_specs=P("ep", "swap"), check_vma=False
    )
```
